128 devices in a mesh: gx: 8 (over x, y_hi), gy: 16 (over z, y_lo, core).
Axes of the slice: x: 4, y: 4 (y_hi: 2, y_lo: 2; y = y_hi * 2 + y_lo), z: 4, core: 2. Of those that a mesh axis runs over, the one named last changes fastest.
Arguments:
- momentum_dist: float32 [19, 64, 256, 512], P(None, 'gx', 'gy'), may hold values from 0.2 to 0.8
- order_dist: float32 [19, 64, 256, 512], P(None, 'gx', 'gy'), may hold values from -0.25 to 0.25
- offsets: int32 [4], replicated, may hold values from 128 to 143, as said below
Outputs:
- next_momentum: float32 [19, 64, 256, 512], P(None, 'gx', 'gy')
- next_order: float32 [19, 64, 256, 512], P(None, 'gx', 'gy')
The draws below stay inside these ranges and needn't reach their ends.
Inputs may be any that keep to these rules, and one draw needn't show every extreme that they name: Every offsets[k] lies from 128 to 143; offsets[0] is 128 and offsets[3] is 143.
All inputs are finite; a program needn't handle non-finite values.
Results may differ from the reference program's by a relative error of at most 0.00002.
Values sent between devices are 32-bit elements; how exact they have to be, the bound alone decides.
A program may use at most 128 MiB of HBM per device.

```python
import jax
import jax.numpy as jnp

CY = 16
NZ = 512
NX = 64
NY = 256


def draw_offsets(key, part):
    key = jax.random.fold_in(key, 5)
    middle_rests = jax.random.randint(key, (2,), 0, CY).astype(jnp.int32)
    remainders = jnp.concatenate([jnp.zeros((1,), jnp.int32), middle_rests, jnp.full((1,), CY - 1, jnp.int32)])
    return (NY // 2 + remainders).astype(jnp.int32)


def steps_of(rng, shape, pieces, low, high):
    level = 1.0
    for axis_at, shards_of in pieces:
        draws = jax.random.uniform(jax.random.fold_in(jax.random.fold_in(rng, 6), axis_at), (shards_of,), jnp.float32, low / len(pieces), high / len(pieces))
        level = level * jnp.repeat(jnp.exp(draws), shape[axis_at] // shards_of).reshape((-1,) + (1,) * (len(shape) - 1 - axis_at))
    return level


def setup_inputs(seed: int = 0) -> dict:
    streams_of = jax.random.split(jax.random.key(seed), 4)
    momentum_dist = jnp.clip(0.2 + 0.6 * jax.random.uniform(streams_of[0], (19, NX, NY, NZ), jnp.float32) ** steps_of(streams_of[0], (19, NX, NY, NZ), ((1, 8), (2, 16)), -0.2, 0.2), 0.2, 0.8)
    order_dist = jnp.clip(jax.random.uniform(streams_of[1], (19, NX, NY, NZ), jnp.float32, -0.25, 0.25) * steps_of(streams_of[1], (19, NX, NY, NZ), ((1, 8), (2, 16)), -0.4, 0.0), -0.25, 0.25)
    offsets = draw_offsets(jax.random.fold_in(streams_of[3], 71), 0)
    return {"momentum_dist": momentum_dist, "order_dist": order_dist, "offsets": offsets}


lattice_velocity = [(0, 0, 0), (1, 0, 0), (-1, 0, 0), (0, 1, 0), (0, -1, 0), (0, 0, 1), (0, 0, -1),
                    (1, 1, 0), (-1, -1, 0), (1, -1, 0), (-1, 1, 0), (1, 0, 1), (-1, 0, -1), (1, 0, -1), (-1, 0, 1),
                    (0, 1, 1), (0, -1, -1), (0, 1, -1), (0, -1, 1)]
lattice_weight = [1.0 / 3.0] + [1.0 / 18.0] * 6 + [1.0 / 36.0] * 12
relax_momentum = 0.8
relax_order = 0.9
bulk_quadratic = -0.0625
bulk_quartic = 0.0625
interface_kappa = 0.04
plane_speed = 0.04
rising = [1, 7, 9, 11, 13]
falling = [2, 8, 10, 12, 14]


def tables(chosen):
    weight = jnp.asarray([lattice_weight[c] for c in chosen], jnp.float32).reshape(-1, 1, 1, 1)
    directions = [jnp.asarray([float(lattice_velocity[c][axis_place]) for c in chosen], jnp.float32).reshape(-1, 1, 1, 1) for axis_place in range(3)]
    return weight, directions


def equilibria(density, order_field, potential, velocity, weight, directions):
    projection = directions[0] * velocity[0] + directions[1] * velocity[1] + directions[2] * velocity[2]
    speed_square = velocity[0] * velocity[0] + velocity[1] * velocity[1] + velocity[2] * velocity[2]
    shape_term = 3.0 * projection + 4.5 * projection * projection - 1.5 * speed_square
    moment_eq = weight * density * (1.0 + shape_term)
    order_eq = weight * (3.0 * potential + order_field * shape_term)
    return moment_eq, order_eq, projection


def collide(momentum, order, order_field, potential, gradient_parts):
    weight, directions = tables(list(range(19)))
    density = jnp.sum(momentum, axis=0)
    force_parts = [potential * part_value for part_value in gradient_parts]
    velocity = [(jnp.sum(directions[axis_place] * momentum, axis=0) + 0.5 * force_parts[axis_place]) / density for axis_place in range(3)]
    moment_eq, order_eq, projection = equilibria(density, order_field, potential, velocity, weight, directions)
    order_eq = jnp.concatenate([(order_field - jnp.sum(order_eq[1:], axis=0))[None], order_eq[1:]], 0)
    force_projection = directions[0] * force_parts[0] + directions[1] * force_parts[1] + directions[2] * force_parts[2]
    velocity_force = velocity[0] * force_parts[0] + velocity[1] * force_parts[1] + velocity[2] * force_parts[2]
    source = (1.0 - 0.5 / relax_momentum) * weight * (3.0 * (force_projection - velocity_force) + 9.0 * projection * force_projection)
    moment_post = momentum - (momentum - moment_eq) / relax_momentum + source
    order_post = order - (order - order_eq) / relax_order
    return moment_post, order_post, moment_eq, order_eq, density, velocity


def jump_terms(chosen, density, order_field, potential, velocity, velocity_jump, base_moment, base_order):
    weight, directions = tables(chosen)
    shifted_velocity = [velocity[0], velocity[1] + velocity_jump, velocity[2]]
    moment_shift, order_shift, projection = equilibria(density, order_field, potential, shifted_velocity, weight, directions)
    return moment_shift - base_moment, order_shift - base_order


def shear_rows(grid_field, shifts, near_weight, far_weight):
    span = grid_field.shape[1]
    positions = jnp.mod(jnp.arange(span, dtype=jnp.int32)[None, :] + shifts[:, None], span).astype(jnp.int32)
    positions = jnp.broadcast_to(positions[:, :, None], grid_field.shape)
    near_values = jnp.take_along_axis(grid_field, positions, axis=1)
    far_values = jnp.take_along_axis(grid_field, jnp.mod(positions + 1, span).astype(jnp.int32), axis=1)
    return near_weight[:, None, None] * near_values + far_weight[:, None, None] * far_values


def reference(momentum_dist, order_dist, offsets):
    quarter = NX // 4
    x_index = jnp.arange(NX, dtype=jnp.int32)
    fractions = (2.0 * jnp.arange(4, dtype=jnp.float32) + 1.0) / 8.0
    lower_mask = x_index % quarter == 0
    lower_plane = (x_index // quarter) % 4
    upper_mask = (x_index + 1) % quarter == 0
    upper_plane = ((x_index + 1) // quarter) % 4
    low_shift = jnp.where(lower_mask, offsets[lower_plane], 0).astype(jnp.int32)
    low_near = jnp.where(lower_mask, 1.0 - fractions[lower_plane], 1.0)
    low_far = jnp.where(lower_mask, fractions[lower_plane], 0.0)
    up_shift = jnp.where(upper_mask, -offsets[upper_plane] - 1, 0).astype(jnp.int32)
    up_near = jnp.where(upper_mask, fractions[upper_plane], 1.0)
    up_far = jnp.where(upper_mask, 1.0 - fractions[upper_plane], 0.0)

    order_field = jnp.sum(order_dist, axis=0)
    order_minus = shear_rows(jnp.roll(order_field, 1, 0), low_shift, low_near, low_far)
    order_plus = shear_rows(jnp.roll(order_field, -1, 0), up_shift, up_near, up_far)
    order_north = jnp.roll(order_field, -1, 1)
    order_south = jnp.roll(order_field, 1, 1)
    order_upper = jnp.roll(order_field, -1, 2)
    order_lower = jnp.roll(order_field, 1, 2)
    laplacian = (order_plus + order_minus) + (order_north + order_south) + (order_upper + order_lower) - 6.0 * order_field
    gradient_parts = [0.5 * (order_plus - order_minus), 0.5 * (order_north - order_south), 0.5 * (order_upper - order_lower)]
    potential = bulk_quadratic * order_field + bulk_quartic * order_field * order_field * order_field - interface_kappa * laplacian

    moment_post, order_post, moment_eq, order_eq, density, velocity = collide(momentum_dist, order_dist, order_field, potential, gradient_parts)

    for chosen, mask, velocity_jump in ((rising, upper_mask, -plane_speed), (falling, lower_mask, plane_speed)):
        moment_delta, order_delta = jump_terms(chosen, density, order_field, potential, velocity, velocity_jump, moment_post[jnp.asarray(chosen)] * 0.0 + moment_eq[jnp.asarray(chosen)], order_eq[jnp.asarray(chosen)])
        row_mask = mask[None, :, None, None]
        moment_post = moment_post.at[jnp.asarray(chosen)].set(jnp.where(row_mask, moment_post[jnp.asarray(chosen)] + moment_delta, moment_post[jnp.asarray(chosen)]))
        order_post = order_post.at[jnp.asarray(chosen)].set(jnp.where(row_mask, order_post[jnp.asarray(chosen)] + order_delta, order_post[jnp.asarray(chosen)]))

    def stream(post):
        arrived = []
        for component in range(19):
            step_x, step_y, step_z = lattice_velocity[component]
            shifted = jnp.roll(post[component], (step_x, step_z), axis=(0, 2))
            if step_x == 1:
                shifted = shear_rows(shifted, low_shift - step_y, low_near, low_far)
            elif step_x == -1:
                shifted = shear_rows(shifted, up_shift - step_y, up_near, up_far)
            else:
                shifted = jnp.roll(shifted, step_y, 1)
            arrived.append(shifted)
        return jnp.stack(arrived)

    return stream(moment_post), stream(order_post)
```

```python
import jax
import jax.numpy as jnp
from jax import lax
from jax.experimental import pallas as pl
from jax.experimental.pallas import tpu as pltpu
from jax.sharding import PartitionSpec as P

lattice_velocity = [
    (0, 0, 0),
    (1, 0, 0),
    (-1, 0, 0),
    (0, 1, 0),
    (0, -1, 0),
    (0, 0, 1),
    (0, 0, -1),
    (1, 1, 0),
    (-1, -1, 0),
    (1, -1, 0),
    (-1, 1, 0),
    (1, 0, 1),
    (-1, 0, -1),
    (1, 0, -1),
    (-1, 0, 1),
    (0, 1, 1),
    (0, -1, -1),
    (0, 1, -1),
    (0, -1, 1),
]
plane_speed = 0.04
rising = [1, 7, 9, 11, 13]
northward = [3, 7, 10, 15, 17]
southward = [4, 8, 9, 16, 18]
level = [c for c in range(19) if lattice_velocity[c][0] == 0]
pairs = [1, 3, 5, 7, 9, 11, 13, 15, 17]
QX, QY, QZ = 8, 16, 512
NGX, NGY = 8, 16
MESH = pl.DeviceIdType.MESH


def axis_sum(direction, parts):
    total = None
    for sign, part in zip(direction, parts):
        if sign == 0:
            continue
        if total is None:
            total = part if sign > 0 else -part
        else:
            total = total + part if sign > 0 else total - part
    return total


def streamed(v, step_y, step_z):
    if step_z:
        v = pltpu.roll(v, step_z % QZ, 1)
    if step_y:
        v = pltpu.roll(v, step_y % QY, 0)
    return v


def step_kernel(
    off_ref, f_hbm, g_hbm, fo, go,
    fin, gin, ph, wp, yps, yp, mm, sb, ob, oc, wb, we, ce, ys, yr,
    load_sem, send_sem, recv_sem,
):
    gx, gy = lax.axis_index("gx"), lax.axis_index("gy")
    odd = lax.rem(gx, 2)
    is_odd = odd == 1
    flat_gx = gx + 1 - 2 * odd
    plane_gx = lax.rem(gx + 2 * odd + NGX - 1, NGX)
    ring = lambda v: lax.rem(v + 2 * NGY, NGY)
    north, south = ring(gy + 1), ring(gy - 1)
    to_a, to_b = ring(gy + 9 - 17 * odd), ring(gy + 8 - 17 * odd)
    to_hi, to_lo = ring(gy + 10 - 17 * odd), ring(gy + 7 - 17 * odd)
    partners = [
        (gx, north), (gx, south),
        (flat_gx, gy), (flat_gx, north), (flat_gx, south),
        (plane_gx, to_a), (plane_gx, to_b), (plane_gx, to_hi), (plane_gx, to_lo),
    ]
    barrier = pltpu.get_barrier_semaphore()
    for partner in partners:
        pl.semaphore_signal(barrier, inc=1, device_id=partner, device_id_type=MESH)

    def load(which, x):
        source, target = ((g_hbm, gin), (f_hbm, fin))[which]
        return pltpu.make_async_copy(source.at[:, x], target.at[:, x], load_sem.at[which, x])

    for which in range(2):
        for x in range(QX):
            load(which, x).start()

    def remote(k, source, target, device):
        return pltpu.make_async_remote_copy(
            src_ref=source, dst_ref=target, send_sem=send_sem.at[k], recv_sem=recv_sem.at[k],
            device_id=device, device_id_type=MESH,
        )

    def phi_row(x, carry):
        load(0, x).wait()
        total = gin[0, x]
        for c in range(1, 19):
            total = total + gin[c, x]
        ph[x + 1] = total
        yps[0, pl.ds(x, 1), :] = total[QY - 1 : QY]
        yps[1, pl.ds(x, 1), :] = total[0:1]
        return carry

    lax.fori_loop(0, QX, phi_row, 0)

    flat_x, plane_x = 7 - 7 * odd, 7 * odd
    phi_copies = [
        remote(0, ph.at[flat_x + 1], ph.at[9 * odd], (flat_gx, gy)),
        remote(1, ph.at[plane_x + 1], wp.at[pl.ds(0, QY)], (plane_gx, to_a)),
        remote(2, ph.at[plane_x + 1], wp.at[pl.ds(QY, QY)], (plane_gx, to_b)),
        remote(3, yps.at[0], yp.at[0], (gx, north)),
        remote(4, yps.at[1], yp.at[1], (gx, south)),
    ]
    pl.semaphore_wait(barrier, len(partners))
    for copy in phi_copies:
        copy.start()

    plane = lax.rem((gx + odd) // 2, 4)
    fraction = (2 * plane + 1).astype(jnp.float32) * 0.125
    near = jnp.where(is_odd, fraction, 1.0 - fraction)
    far = 1.0 - near
    rest = off_ref[plane] - 8 * QY
    first = jnp.where(is_odd, QY - 1 - rest, rest)

    def interpolated(window, start):
        count = window.shape[0]
        here = pltpu.roll(window, lax.rem(count - start, count), 0)
        return near * here[:QY] + far * pltpu.roll(here, count - 1, 0)[:QY]

    row_y = lax.broadcasted_iota(jnp.int32, (QY, QZ), 0)

    def gradients(x):
        centre, minus, plus = ph[x + 1], ph[x], ph[x + 2]
        south_v = jnp.where(row_y == 0, yp[0, pl.ds(x, 1), :], pltpu.roll(centre, 1, 0))
        north_v = jnp.where(row_y == QY - 1, yp[1, pl.ds(x, 1), :], pltpu.roll(centre, QY - 1, 0))
        upper, lower = pltpu.roll(centre, QZ - 1, 1), pltpu.roll(centre, 1, 1)
        lap = (plus + minus) + (north_v + south_v) + (upper + lower) - 6.0 * centre
        mu = centre * (0.0625 * centre * centre - 0.0625) - 0.04 * lap
        half = 0.5 * mu
        mm[0] = mu
        mm[1] = half * (plus - minus)
        mm[2] = half * (north_v - south_v)
        mm[3] = half * (upper - lower)

    def collide_row(x, face):
        gradients(x)
        if face is not None:
            top = odd == face
            sign = jnp.where(top, 1.0, -1.0)
            jump = sign * (-plane_speed)

        def chunk(step, carry):
            zs = pl.ds(pl.multiple_of(step * 128, 128), 128)
            for h in range(2):
                rows = pl.ds(8 * h, 8)
                read = lambda ref, c: ref[c, x, rows, zs]
                f = [read(fin, c) for c in range(19)]
                phi = ph[x + 1, rows, zs]
                mu = mm[0, rows, zs]
                force = [mm[a, rows, zs] for a in (1, 2, 3)]
                diff = {c: f[c] - f[c + 1] for c in pairs}
                rho = f[0]
                for c in pairs:
                    rho = rho + (f[c] + f[c + 1])
                inverse = 1.0 / rho
                velocity = []
                for a in range(3):
                    total = 0.5 * force[a]
                    for c in pairs:
                        s = lattice_velocity[c][a]
                        if s:
                            total = total + diff[c] if s > 0 else total - diff[c]
                    velocity.append(total * inverse)
                ux, uy, uz = velocity
                u2 = ux * ux + uy * uy + uz * uz
                uf = ux * force[0] + uy * force[1] + uz * force[2]
                base = 1.25 * rho * (1.0 - 1.5 * u2) - 1.125 * uf
                scale = 5.625 * rho
                pull = [3.375 * part for part in force]
                gbase = (10.0 / 9.0) * (3.0 * mu - 1.5 * phi * u2)
                gscale = 5.0 * phi
                fin[0, x, rows, zs] = (1.0 / 3.0) * base - 0.25 * f[0]
                gin[0, x, rows, zs] = (10.0 / 9.0) * (phi - 2.0 * mu - 0.5 * phi * u2) - (
                    1.0 / 9.0
                ) * read(gin, 0)
                if face == 1:
                    common = -3.0 * uy - 1.5 * jump
                    wrho, wphi = jump * rho, jump * phi
                for c in pairs:
                    w = 1.0 / 18.0 if c < 7 else 1.0 / 36.0
                    direction = lattice_velocity[c]
                    p = axis_sum(direction, velocity)
                    b = axis_sum(direction, pull)
                    a = scale * p
                    ab = a + b
                    even = w * (base + p * ab)
                    oddpart = (w / 3.0) * (a + ab)
                    f_up = (even + oddpart) - 0.25 * f[c]
                    f_down = (even - oddpart) - 0.25 * f[c + 1]
                    h_p = gscale * p
                    geven = w * (gbase + p * h_p)
                    godd = (2.0 * w / 3.0) * h_p
                    g_up = (geven + godd) - (1.0 / 9.0) * read(gin, c)
                    g_down = (geven - godd) - (1.0 / 9.0) * read(gin, c + 1)
                    fin[c, x, rows, zs] = f_up
                    fin[c + 1, x, rows, zs] = f_down
                    gin[c, x, rows, zs] = g_up
                    gin[c + 1, x, rows, zs] = g_down
                    if face is not None and c in rising:
                        j = rising.index(c)
                        f_sent = jnp.where(top, f_up, f_down)
                        g_sent = jnp.where(top, g_up, g_down)
                        if face == 1:
                            cy = float(direction[1])
                            delta = common
                            if cy:
                                delta = delta + (cy * 9.0 * p + (cy * 3.0 * sign + 4.5 * jump))
                            f_sent = f_sent + w * (wrho * delta)
                            g_sent = g_sent + w * (wphi * delta)
                        sb[face, j, rows, zs] = f_sent
                        sb[face, 5 + j, rows, zs] = g_sent
            return carry

        lax.fori_loop(0, QZ // 128, chunk, 0)
        slot = jnp.where(top, 1, 0) if face is not None else x + 1
        group, line = slot // 4, lax.rem(slot, 4) * 10
        for d, chosen, y in ((0, northward, QY - 1), (1, southward, 0)):
            for j, c in enumerate(chosen):
                ys[d, group, pl.ds(line + j, 1), :] = fin[c, x, y : y + 1, :]
                ys[d, group, pl.ds(line + 5 + j, 1), :] = gin[c, x, y : y + 1, :]
        if face is not None:
            j_hi = jnp.where(top, 1, 2)
            for family in range(2):
                ce[face, 0, family : family + 1, :] = sb[face, j_hi + 5 * family, QY - 1 : QY, :]
                ce[face, 1, family : family + 1, :] = sb[face, 3 - j_hi + 5 * family, 0:1, :]

    def wait_f(x, carry):
        load(1, x).wait()
        return carry

    lax.fori_loop(0, QX, wait_f, 0)

    for copy in (phi_copies[0], phi_copies[3], phi_copies[4]):
        copy.wait_recv()
    collide_row(flat_x, 0)
    flat_copies = [
        remote(5, sb.at[0], ob, (flat_gx, gy)),
        remote(6, ce.at[0, 0], oc.at[0], (flat_gx, north)),
        remote(7, ce.at[0, 1], oc.at[1], (flat_gx, south)),
    ]
    for copy in flat_copies:
        copy.start()
    phi_copies[1].wait_recv()
    phi_copies[2].wait_recv()
    ph[9 * odd] = interpolated(wp[...], first)
    collide_row(plane_x, 1)
    plane_copies = [
        remote(8, ce.at[1, 0], we.at[0], (plane_gx, to_hi)),
        remote(9, ce.at[1, 1], we.at[1], (plane_gx, to_lo)),
        remote(10, sb.at[1], wb.at[:, pl.ds(8, QY)], (plane_gx, to_a)),
        remote(11, sb.at[1], wb.at[:, pl.ds(8 + QY, QY)], (plane_gx, to_b)),
    ]
    for copy in plane_copies:
        copy.start()

    def inner_row(x, carry):
        collide_row(x, None)
        return carry

    side_copies = [
        remote(12 + 2 * d + group, ys.at[d, group], yr.at[d, group], (gx, (north, south)[d]))
        for group in range(2)
        for d in range(2)
    ]
    lax.fori_loop(1, 3, inner_row, 0)
    side_copies[0].start()
    side_copies[1].start()
    lax.fori_loop(3, QX - 1, inner_row, 0)
    side_copies[2].start()
    side_copies[3].start()

    families = ((fin, fo), (gin, go))

    def stream_level(x, carry):
        for source, target in families:
            for c in level:
                target[c, x] = streamed(source[c, x], *lattice_velocity[c][1:])
        return carry

    def stream_across(x, carry):
        for source, target in families:
            for c in rising:
                _, step_y, step_z = lattice_velocity[c]
                target[c, x + 1] = streamed(source[c, x], step_y, step_z)
                target[c + 1, x] = streamed(source[c + 1, x + 1], -step_y, -step_z)
        return carry

    lax.fori_loop(0, QX, stream_level, 0)
    lax.fori_loop(0, QX - 1, stream_across, 0)

    for copy in side_copies:
        copy.wait_recv()

    def side_line(x):
        slot = jnp.where(x == 0, 0, jnp.where(x == QX - 1, 1, x + 1))
        return slot // 4, lax.rem(slot, 4) * 10

    def side_rows(x, chosen_x, shift):
        group, line = side_line(x)
        for d, chosen, y in ((0, northward, 0), (1, southward, QY - 1)):
            for j, c in enumerate(chosen):
                step_x, _, step_z = lattice_velocity[c]
                if step_x != chosen_x:
                    continue
                for family in range(2):
                    row = yr[d, group, pl.ds(line + 5 * family + j, 1), :]
                    if step_z:
                        row = pltpu.roll(row, step_z % QZ, 1)
                    families[family][1][c, x + shift, y : y + 1, :] = row

    def side_level(x, carry):
        side_rows(x, 0, 0)
        return carry

    def side_across(x, carry):
        side_rows(x, 1, 1)
        side_rows(x + 1, -1, -1)
        return carry

    lax.fori_loop(0, QX, side_level, 0)
    lax.fori_loop(0, QX - 1, side_across, 0)

    for copy in flat_copies:
        copy.wait_recv()

    def arrive_flat(sign, x):
        for j, c in enumerate(rising):
            step_y, step_z = sign * lattice_velocity[c][1], sign * lattice_velocity[c][2]
            c = c if sign > 0 else c + 1
            for family in range(2):
                v = streamed(ob[5 * family + j], step_y, step_z)
                if step_y > 0:
                    v = jnp.where(row_y == 0, oc[0, family : family + 1, :], v)
                elif step_y < 0:
                    v = jnp.where(row_y == QY - 1, oc[1, family : family + 1, :], v)
                families[family][1][c, x] = v

    pl.when(is_odd)(lambda: arrive_flat(1, 0))
    pl.when(jnp.logical_not(is_odd))(lambda: arrive_flat(-1, QX - 1))

    for copy in plane_copies:
        copy.wait_recv()

    def arrive_plane(sign, x):
        for j, c in enumerate(rising):
            step_y, step_z = sign * lattice_velocity[c][1], sign * lattice_velocity[c][2]
            c = c if sign > 0 else c + 1
            for family in range(2):
                k = 5 * family + j
                if step_y > 0:
                    wb[k, 7:8, :] = we[0, family : family + 1, :]
                elif step_y < 0:
                    wb[k, 8 + 2 * QY : 9 + 2 * QY, :] = we[1, family : family + 1, :]
                v = interpolated(wb[k], first + (8 - step_y))
                families[family][1][c, x] = streamed(v, 0, step_z)

    pl.when(jnp.logical_not(is_odd))(lambda: arrive_plane(1, 0))
    pl.when(is_odd)(lambda: arrive_plane(-1, QX - 1))

    for copy in phi_copies + flat_copies + plane_copies + side_copies:
        copy.wait_send()


def on_device(momentum_dist, order_dist, offsets):
    block = (19, QX, QY, QZ)
    f32 = jnp.float32
    vmem = pl.BlockSpec(memory_space=pltpu.VMEM)
    return pl.pallas_call(
        step_kernel,
        out_shape=(pltpu.VMEM(block, f32), pltpu.VMEM(block, f32)),
        in_specs=[
            pl.BlockSpec(memory_space=pltpu.SMEM),
            pl.BlockSpec(memory_space=pltpu.HBM),
            pl.BlockSpec(memory_space=pltpu.HBM),
        ],
        out_specs=(vmem, vmem),
        scratch_shapes=[
            pltpu.VMEM(block, f32),
            pltpu.VMEM(block, f32),
            pltpu.VMEM((QX + 2, QY, QZ), f32),
            pltpu.VMEM((2 * QY, QZ), f32),
            pltpu.VMEM((2, QX, QZ), f32),
            pltpu.VMEM((2, QX, QZ), f32),
            pltpu.VMEM((4, QY, QZ), f32),
            pltpu.VMEM((2, 10, QY, QZ), f32),
            pltpu.VMEM((10, QY, QZ), f32),
            pltpu.VMEM((2, 8, QZ), f32),
            pltpu.VMEM((10, 2 * QY + 16, QZ), f32),
            pltpu.VMEM((2, 8, QZ), f32),
            pltpu.VMEM((2, 2, 8, QZ), f32),
            pltpu.VMEM((2, 2, 40, QZ), f32),
            pltpu.VMEM((2, 2, 40, QZ), f32),
            pltpu.SemaphoreType.DMA((2, QX)),
            pltpu.SemaphoreType.DMA((16,)),
            pltpu.SemaphoreType.DMA((16,)),
        ],
        compiler_params=pltpu.CompilerParams(
            collective_id=0, has_side_effects=True, vmem_limit_bytes=40 * 2**20
        ),
    )(
        offsets,
        pltpu.with_memory_space_constraint(momentum_dist, pltpu.HBM),
        pltpu.with_memory_space_constraint(order_dist, pltpu.HBM),
    )


def solution(mesh):
    return jax.shard_map(
        on_device,
        mesh=mesh,
        in_specs=(P(None, "gx", "gy", None), P(None, "gx", "gy", None), P()),
        out_specs=(P(None, "gx", "gy", None), P(None, "gx", "gy", None)),
        check_vma=False,
    )
```

```python
import jax
import jax.numpy as jnp
from jax import lax
from jax.experimental import pallas as pl
from jax.experimental.pallas import tpu as pltpu
from jax.sharding import PartitionSpec as P

lattice_velocity = [
    (0, 0, 0),
    (1, 0, 0),
    (-1, 0, 0),
    (0, 1, 0),
    (0, -1, 0),
    (0, 0, 1),
    (0, 0, -1),
    (1, 1, 0),
    (-1, -1, 0),
    (1, -1, 0),
    (-1, 1, 0),
    (1, 0, 1),
    (-1, 0, -1),
    (1, 0, -1),
    (-1, 0, 1),
    (0, 1, 1),
    (0, -1, -1),
    (0, 1, -1),
    (0, -1, 1),
]
plane_speed = 0.04
rising = [1, 7, 9, 11, 13]
northward = [3, 7, 10, 15, 17]
southward = [4, 8, 9, 16, 18]
level = [c for c in range(19) if lattice_velocity[c][0] == 0]
pairs = [1, 3, 5, 7, 9, 11, 13, 15, 17]
QX, QY, QZ = 8, 16, 512
NGX, NGY = 8, 16
MESH = pl.DeviceIdType.MESH


def axis_sum(direction, parts):
    total = None
    for sign, part in zip(direction, parts):
        if sign == 0:
            continue
        if total is None:
            total = part if sign > 0 else -part
        else:
            total = total + part if sign > 0 else total - part
    return total


def streamed(v, step_y, step_z):
    if step_z:
        v = pltpu.roll(v, step_z % QZ, 1)
    if step_y:
        v = pltpu.roll(v, step_y % QY, 0)
    return v


def step_kernel(
    off_hbm, f_hbm, g_hbm, fo, go,
    off_ref, fin, gin, ph, wp, yps, yp, mm, sb, ob, oc, wb, we, ce, ys, yr,
    load_sem, off_sem, send_sem, recv_sem,
):
    gx, gy = lax.axis_index("gx"), lax.axis_index("gy")
    odd = lax.rem(gx, 2)
    is_odd = odd == 1
    flat_gx = gx + 1 - 2 * odd
    plane_gx = lax.rem(gx + 2 * odd + NGX - 1, NGX)
    ring = lambda v: lax.rem(v + 2 * NGY, NGY)
    north, south = ring(gy + 1), ring(gy - 1)
    main_gy, extra_gy = ring(gy + 8), ring(gy + 9 - 18 * odd)
    core_gy = gy + 1 - 2 * lax.rem(gy, 2)
    sends_twice = lax.rem(gx + gy, 2) == 1
    to_hi, to_lo = ring(gy + 10 - 17 * odd), ring(gy + 7 - 17 * odd)
    partners = [
        (gx, north), (gx, south),
        (flat_gx, gy), (flat_gx, north), (flat_gx, south),
        (plane_gx, main_gy), (plane_gx, extra_gy), (plane_gx, to_hi), (plane_gx, to_lo),
    ]
    barrier = pltpu.get_barrier_semaphore()
    for partner in partners:
        pl.semaphore_signal(barrier, inc=1, device_id=partner, device_id_type=MESH)

    def load(which, x):
        source, target = ((g_hbm, gin), (f_hbm, fin))[which]
        return pltpu.make_async_copy(source.at[:, x], target.at[:, x], load_sem.at[which, x])

    for which in range(2):
        for x in (0, QX - 1, *range(1, QX - 1)):
            load(which, x).start()
    load_offsets = pltpu.make_async_copy(off_hbm, off_ref, off_sem)
    load_offsets.start()

    def remote(k, source, target, device):
        return pltpu.make_async_remote_copy(
            src_ref=source, dst_ref=target, send_sem=send_sem.at[k], recv_sem=recv_sem.at[k],
            device_id=device, device_id_type=MESH,
        )

    def phi_row(x, carry):
        load(0, x).wait()
        total = gin[0, x]
        for c in range(1, 19):
            total = total + gin[c, x]
        ph[x + 1] = total
        yps[0, pl.ds(x, 1), :] = total[QY - 1 : QY]
        yps[1, pl.ds(x, 1), :] = total[0:1]
        return carry

    phi_row(0, 0)
    phi_row(QX - 1, 0)
    flat_x, plane_x = 7 - 7 * odd, 7 * odd
    main_slot = 1 - odd
    phi_copies = [
        remote(0, ph.at[flat_x + 1], ph.at[9 * odd], (flat_gx, gy)),
        remote(1, ph.at[plane_x + 1], wp.at[main_slot], (plane_gx, main_gy)),
        remote(2, ph.at[plane_x + 1], wp.at[1 - main_slot], (plane_gx, extra_gy)),
        remote(3, yps.at[0], yp.at[0], (gx, north)),
        remote(4, yps.at[1], yp.at[1], (gx, south)),
    ]
    pl.semaphore_wait(barrier, len(partners))
    for copy in phi_copies[:3]:
        copy.start()
    lax.fori_loop(1, QX - 1, phi_row, 0)
    for copy in phi_copies[3:]:
        copy.start()

    load_offsets.wait()
    plane = lax.rem((gx + odd) // 2, 4)
    fraction = (2 * plane + 1).astype(jnp.float32) * 0.125
    near = jnp.where(is_odd, fraction, 1.0 - fraction)
    far = 1.0 - near
    rest = off_ref[plane] - 8 * QY
    first = jnp.where(is_odd, QY - 1 - rest, rest)

    def interpolated(window, start):
        count = window.shape[0]
        here = pltpu.roll(window, lax.rem(count - start, count), 0)
        return near * here[:QY] + far * pltpu.roll(here, count - 1, 0)[:QY]

    row_y = lax.broadcasted_iota(jnp.int32, (QY, QZ), 0)

    def gradients(x):
        centre, minus, plus = ph[x + 1], ph[x], ph[x + 2]
        south_v = jnp.where(row_y == 0, yp[0, pl.ds(x, 1), :], pltpu.roll(centre, 1, 0))
        north_v = jnp.where(row_y == QY - 1, yp[1, pl.ds(x, 1), :], pltpu.roll(centre, QY - 1, 0))
        upper, lower = pltpu.roll(centre, QZ - 1, 1), pltpu.roll(centre, 1, 1)
        lap = (plus + minus) + (north_v + south_v) + (upper + lower) - 6.0 * centre
        mu = centre * (0.0625 * centre * centre - 0.0625) - 0.04 * lap
        half = 0.5 * mu
        mm[0] = mu
        mm[1] = half * (plus - minus)
        mm[2] = half * (north_v - south_v)
        mm[3] = half * (upper - lower)

    def collide_row(x, face):
        gradients(x)
        if face is not None:
            top = odd == face
            sign = jnp.where(top, 1.0, -1.0)
            jump = sign * (-plane_speed)

        def chunk(step, carry):
            zs = pl.ds(pl.multiple_of(step * 128, 128), 128)
            for h in range(2):
                rows = pl.ds(8 * h, 8)
                read = lambda ref, c: ref[c, x, rows, zs]
                f = [read(fin, c) for c in range(19)]
                phi = ph[x + 1, rows, zs]
                mu = mm[0, rows, zs]
                force = [mm[a, rows, zs] for a in (1, 2, 3)]
                diff = {c: f[c] - f[c + 1] for c in pairs}
                rho = f[0]
                for c in pairs:
                    rho = rho + (f[c] + f[c + 1])
                inverse = 1.0 / rho
                velocity = []
                for a in range(3):
                    total = 0.5 * force[a]
                    for c in pairs:
                        s = lattice_velocity[c][a]
                        if s:
                            total = total + diff[c] if s > 0 else total - diff[c]
                    velocity.append(total * inverse)
                ux, uy, uz = velocity
                u2 = ux * ux + uy * uy + uz * uz
                uf = ux * force[0] + uy * force[1] + uz * force[2]
                base = 1.25 * rho * (1.0 - 1.5 * u2) - 1.125 * uf
                scale = 5.625 * rho
                pull = [3.375 * part for part in force]
                gbase = (10.0 / 9.0) * (3.0 * mu - 1.5 * phi * u2)
                gscale = 5.0 * phi
                fin[0, x, rows, zs] = (1.0 / 3.0) * base - 0.25 * f[0]
                gin[0, x, rows, zs] = (10.0 / 9.0) * (phi - 2.0 * mu - 0.5 * phi * u2) - (
                    1.0 / 9.0
                ) * read(gin, 0)
                if face == 1:
                    common = -3.0 * uy - 1.5 * jump
                    wrho, wphi = jump * rho, jump * phi
                for c in pairs:
                    w = 1.0 / 18.0 if c < 7 else 1.0 / 36.0
                    direction = lattice_velocity[c]
                    p = axis_sum(direction, velocity)
                    b = axis_sum(direction, pull)
                    a = scale * p
                    ab = a + b
                    even = w * (base + p * ab)
                    oddpart = (w / 3.0) * (a + ab)
                    f_up = (even + oddpart) - 0.25 * f[c]
                    f_down = (even - oddpart) - 0.25 * f[c + 1]
                    h_p = gscale * p
                    geven = w * (gbase + p * h_p)
                    godd = (2.0 * w / 3.0) * h_p
                    g_up = (geven + godd) - (1.0 / 9.0) * read(gin, c)
                    g_down = (geven - godd) - (1.0 / 9.0) * read(gin, c + 1)
                    fin[c, x, rows, zs] = f_up
                    fin[c + 1, x, rows, zs] = f_down
                    gin[c, x, rows, zs] = g_up
                    gin[c + 1, x, rows, zs] = g_down
                    if face is not None and c in rising:
                        j = rising.index(c)
                        f_sent = jnp.where(top, f_up, f_down)
                        g_sent = jnp.where(top, g_up, g_down)
                        if face == 1:
                            cy = float(direction[1])
                            delta = common
                            if cy:
                                delta = delta + (cy * 9.0 * p + (cy * 3.0 * sign + 4.5 * jump))
                            f_sent = f_sent + w * (wrho * delta)
                            g_sent = g_sent + w * (wphi * delta)
                        sb[face, j, rows, zs] = f_sent
                        sb[face, 5 + j, rows, zs] = g_sent
            return carry

        lax.fori_loop(0, QZ // 128, chunk, 0)
        slot = jnp.where(top, 1, 0) if face is not None else x + 1
        group, line = slot // 4, lax.rem(slot, 4) * 10
        for d, chosen, y in ((0, northward, QY - 1), (1, southward, 0)):
            for j, c in enumerate(chosen):
                ys[d, group, pl.ds(line + j, 1), :] = fin[c, x, y : y + 1, :]
                ys[d, group, pl.ds(line + 5 + j, 1), :] = gin[c, x, y : y + 1, :]
        if face is not None:
            j_hi = jnp.where(top, 1, 2)
            for family in range(2):
                ce[face, 0, family : family + 1, :] = sb[face, j_hi + 5 * family, QY - 1 : QY, :]
                ce[face, 1, family : family + 1, :] = sb[face, 3 - j_hi + 5 * family, 0:1, :]

    def wait_f(x, carry):
        load(1, x).wait()
        return carry

    lax.fori_loop(0, QX, wait_f, 0)

    for copy in (phi_copies[0], phi_copies[3], phi_copies[4]):
        copy.wait_recv()
    collide_row(flat_x, 0)
    flat_copies = [
        remote(5, sb.at[0], ob, (flat_gx, gy)),
        remote(6, ce.at[0, 0], oc.at[0], (flat_gx, north)),
        remote(7, ce.at[0, 1], oc.at[1], (flat_gx, south)),
    ]
    for copy in flat_copies:
        copy.start()
    phi_copies[1].wait_recv()
    phi_copies[2].wait_recv()
    ph[9 * odd] = interpolated(wp[...].reshape(2 * QY, QZ), first)
    collide_row(plane_x, 1)
    plane_copies = [
        remote(8, ce.at[1, 0], we.at[0], (plane_gx, to_hi)),
        remote(9, ce.at[1, 1], we.at[1], (plane_gx, to_lo)),
    ]
    rows_at = lambda half, slot: wb.at[pl.ds(5 * half, 5), pl.ds(8 + QY * slot, QY)]
    layer = lambda half: sb.at[1, pl.ds(5 * half, 5)]
    main_copies = [
        remote(10 + half, layer(half), rows_at(half, main_slot), (plane_gx, main_gy))
        for half in range(2)
    ]
    extra_copies = [
        remote(16 + half, layer(half), rows_at(half, 1 - main_slot), (plane_gx, extra_gy))
        for half in range(2)
    ]
    hand_on = [
        pltpu.make_async_remote_copy(
            src_ref=rows_at(half, odd), dst_ref=rows_at(half, 1 - odd),
            send_sem=send_sem.at[18 + half], recv_sem=recv_sem.at[16 + half],
            device_id=(gx, core_gy), device_id_type=MESH,
        )
        for half in range(2)
    ]
    for copy in plane_copies + main_copies:
        copy.start()

    @pl.when(sends_twice)
    def _():
        for copy in extra_copies:
            copy.start()

    def inner_row(x, carry):
        collide_row(x, None)
        return carry

    side_copies = [
        remote(12 + 2 * d + group, ys.at[d, group], yr.at[d, group], (gx, (north, south)[d]))
        for group in range(2)
        for d in range(2)
    ]
    lax.fori_loop(1, 3, inner_row, 0)
    side_copies[0].start()
    side_copies[1].start()
    lax.fori_loop(3, QX - 1, inner_row, 0)
    side_copies[2].start()
    side_copies[3].start()

    families = ((fin, fo), (gin, go))

    def stream_level(x, carry):
        for source, target in families:
            for c in level:
                target[c, x] = streamed(source[c, x], *lattice_velocity[c][1:])
        return carry

    def stream_across(x, carry):
        for source, target in families:
            for c in rising:
                _, step_y, step_z = lattice_velocity[c]
                target[c, x + 1] = streamed(source[c, x], step_y, step_z)
                target[c + 1, x] = streamed(source[c + 1, x + 1], -step_y, -step_z)
        return carry

    lax.fori_loop(0, QX, stream_level, 0)
    lax.fori_loop(0, QX - 1, stream_across, 0)

    for copy in side_copies:
        copy.wait_recv()

    def side_line(x):
        slot = jnp.where(x == 0, 0, jnp.where(x == QX - 1, 1, x + 1))
        return slot // 4, lax.rem(slot, 4) * 10

    def side_rows(x, chosen_x, shift):
        group, line = side_line(x)
        for d, chosen, y in ((0, northward, 0), (1, southward, QY - 1)):
            for j, c in enumerate(chosen):
                step_x, _, step_z = lattice_velocity[c]
                if step_x != chosen_x:
                    continue
                for family in range(2):
                    row = yr[d, group, pl.ds(line + 5 * family + j, 1), :]
                    if step_z:
                        row = pltpu.roll(row, step_z % QZ, 1)
                    families[family][1][c, x + shift, y : y + 1, :] = row

    def side_level(x, carry):
        side_rows(x, 0, 0)
        return carry

    def side_across(x, carry):
        side_rows(x, 1, 1)
        side_rows(x + 1, -1, -1)
        return carry

    lax.fori_loop(0, QX, side_level, 0)
    lax.fori_loop(0, QX - 1, side_across, 0)

    for copy in flat_copies:
        copy.wait_recv()

    def arrive_flat(sign, x):
        for j, c in enumerate(rising):
            step_y, step_z = sign * lattice_velocity[c][1], sign * lattice_velocity[c][2]
            c = c if sign > 0 else c + 1
            for family in range(2):
                v = streamed(ob[5 * family + j], step_y, step_z)
                if step_y > 0:
                    v = jnp.where(row_y == 0, oc[0, family : family + 1, :], v)
                elif step_y < 0:
                    v = jnp.where(row_y == QY - 1, oc[1, family : family + 1, :], v)
                families[family][1][c, x] = v

    pl.when(is_odd)(lambda: arrive_flat(1, 0))
    pl.when(jnp.logical_not(is_odd))(lambda: arrive_flat(-1, QX - 1))

    for half in range(2):
        main_copies[half].wait_recv()
        pl.when(sends_twice)(hand_on[half].start)
    for copy in plane_copies + extra_copies:
        copy.wait_recv()

    def arrive_plane(sign, x):
        for j, c in enumerate(rising):
            step_y, step_z = sign * lattice_velocity[c][1], sign * lattice_velocity[c][2]
            c = c if sign > 0 else c + 1
            for family in range(2):
                k = 5 * family + j
                if step_y > 0:
                    wb[k, 7:8, :] = we[0, family : family + 1, :]
                elif step_y < 0:
                    wb[k, 8 + 2 * QY : 9 + 2 * QY, :] = we[1, family : family + 1, :]
                v = interpolated(wb[k], first + (8 - step_y))
                families[family][1][c, x] = streamed(v, 0, step_z)

    pl.when(jnp.logical_not(is_odd))(lambda: arrive_plane(1, 0))
    pl.when(is_odd)(lambda: arrive_plane(-1, QX - 1))

    for copy in phi_copies + flat_copies + plane_copies + main_copies + side_copies:
        copy.wait_send()

    @pl.when(sends_twice)
    def _():
        for copy in extra_copies + hand_on:
            copy.wait_send()


def write_kernel(f, g, f_hbm, g_hbm, sem):
    copies = [
        pltpu.make_async_copy(source.at[:, x], target.at[:, x], sem.at[which, x])
        for x in range(QX)
        for which, (source, target) in enumerate(((f, f_hbm), (g, g_hbm)))
    ]
    for copy in copies:
        copy.start()
    for copy in copies:
        copy.wait()


def on_device(momentum_dist, order_dist, offsets):
    block = (19, QX, QY, QZ)
    f32 = jnp.float32
    vmem, hbm = pl.BlockSpec(memory_space=pltpu.VMEM), pl.BlockSpec(memory_space=pltpu.HBM)
    f_new, g_new = pl.pallas_call(
        step_kernel,
        out_shape=(pltpu.VMEM(block, f32), pltpu.VMEM(block, f32)),
        in_specs=[hbm, hbm, hbm],
        out_specs=(vmem, vmem),
        scratch_shapes=[
            pltpu.SMEM((4,), jnp.int32),
            pltpu.VMEM(block, f32),
            pltpu.VMEM(block, f32),
            pltpu.VMEM((QX + 2, QY, QZ), f32),
            pltpu.VMEM((2, QY, QZ), f32),
            pltpu.VMEM((2, QX, QZ), f32),
            pltpu.VMEM((2, QX, QZ), f32),
            pltpu.VMEM((4, QY, QZ), f32),
            pltpu.VMEM((2, 10, QY, QZ), f32),
            pltpu.VMEM((10, QY, QZ), f32),
            pltpu.VMEM((2, 2, QZ), f32),
            pltpu.VMEM((10, 2 * QY + 16, QZ), f32),
            pltpu.VMEM((2, 2, QZ), f32),
            pltpu.VMEM((2, 2, 2, QZ), f32),
            pltpu.VMEM((2, 2, 40, QZ), f32),
            pltpu.VMEM((2, 2, 40, QZ), f32),
            pltpu.SemaphoreType.DMA((2, QX)),
            pltpu.SemaphoreType.DMA,
            pltpu.SemaphoreType.DMA((20,)),
            pltpu.SemaphoreType.DMA((18,)),
        ],
        compiler_params=pltpu.CompilerParams(
            collective_id=0, has_side_effects=True, vmem_limit_bytes=32 * 2**20
        ),
    )(
        *(
            pltpu.with_memory_space_constraint(operand, pltpu.HBM)
            for operand in (offsets, momentum_dist, order_dist)
        )
    )
    whole = jax.ShapeDtypeStruct(block, f32)
    return pl.pallas_call(
        write_kernel,
        out_shape=(whole, whole),
        in_specs=[vmem, vmem],
        out_specs=(hbm, hbm),
        scratch_shapes=[pltpu.SemaphoreType.DMA((2, QX))],
        compiler_params=pltpu.CompilerParams(vmem_limit_bytes=4 * 2**20),
    )(
        pltpu.with_memory_space_constraint(f_new, pltpu.VMEM),
        pltpu.with_memory_space_constraint(g_new, pltpu.VMEM),
    )


def solution(mesh):
    return jax.shard_map(
        on_device,
        mesh=mesh,
        in_specs=(P(None, "gx", "gy", None), P(None, "gx", "gy", None), P()),
        out_specs=(P(None, "gx", "gy", None), P(None, "gx", "gy", None)),
        check_vma=False,
    )
```

```python
import jax
import jax.numpy as jnp
from jax import lax
from jax.experimental import pallas as pl
from jax.experimental.pallas import tpu as pltpu
from jax.sharding import PartitionSpec as P

lattice_velocity = [
    (0, 0, 0),
    (1, 0, 0),
    (-1, 0, 0),
    (0, 1, 0),
    (0, -1, 0),
    (0, 0, 1),
    (0, 0, -1),
    (1, 1, 0),
    (-1, -1, 0),
    (1, -1, 0),
    (-1, 1, 0),
    (1, 0, 1),
    (-1, 0, -1),
    (1, 0, -1),
    (-1, 0, 1),
    (0, 1, 1),
    (0, -1, -1),
    (0, 1, -1),
    (0, -1, 1),
]
plane_speed = 0.04
rising = [1, 7, 9, 11, 13]
northward = [3, 7, 10, 15, 17]
southward = [4, 8, 9, 16, 18]
level = [c for c in range(19) if lattice_velocity[c][0] == 0]
pairs = [1, 3, 5, 7, 9, 11, 13, 15, 17]
QX, QY, QZ = 8, 16, 512
NGX, NGY = 8, 16
MESH = pl.DeviceIdType.MESH


def axis_sum(direction, parts):
    total = None
    for sign, part in zip(direction, parts):
        if sign == 0:
            continue
        if total is None:
            total = part if sign > 0 else -part
        else:
            total = total + part if sign > 0 else total - part
    return total


def streamed(v, step_y, step_z):
    if step_z:
        v = pltpu.roll(v, step_z % QZ, 1)
    if step_y:
        v = pltpu.roll(v, step_y % QY, 0)
    return v


def step_kernel(
    off_hbm, f_hbm, g_hbm, fo, go,
    off_ref, fin, gin, ph, wp, yps, yp, mm, sb, ob, oc, wb, we, ce, ys, yr,
    load_sem, off_sem, send_sem, recv_sem,
):
    gx, gy = lax.axis_index("gx"), lax.axis_index("gy")
    odd = lax.rem(gx, 2)
    is_odd = odd == 1
    flat_gx = gx + 1 - 2 * odd
    plane_gx = lax.rem(gx + 2 * odd + NGX - 1, NGX)
    ring = lambda v: lax.rem(v + 2 * NGY, NGY)
    north, south = ring(gy + 1), ring(gy - 1)
    main_gy, extra_gy = ring(gy + 8), ring(gy + 9 - 18 * odd)
    core_gy = gy + 1 - 2 * lax.rem(gy, 2)
    sends_twice = lax.rem(gx + gy, 2) == 1
    to_hi, to_lo = ring(gy + 10 - 17 * odd), ring(gy + 7 - 17 * odd)
    partners = [
        (gx, north), (gx, south),
        (flat_gx, gy), (flat_gx, north), (flat_gx, south),
        (plane_gx, main_gy), (plane_gx, extra_gy), (plane_gx, to_hi), (plane_gx, to_lo),
    ]
    barrier = pltpu.get_barrier_semaphore()
    for partner in partners:
        pl.semaphore_signal(barrier, inc=1, device_id=partner, device_id_type=MESH)

    def load(which, x):
        source, target = ((g_hbm, gin), (f_hbm, fin))[which]
        return pltpu.make_async_copy(source.at[:, x], target.at[:, x], load_sem.at[which, x])

    for which in range(2):
        for x in (0, QX - 1, *range(1, QX - 1)):
            load(which, x).start()
    load_offsets = pltpu.make_async_copy(off_hbm, off_ref, off_sem)
    load_offsets.start()

    def remote(k, source, target, device):
        return pltpu.make_async_remote_copy(
            src_ref=source, dst_ref=target, send_sem=send_sem.at[k], recv_sem=recv_sem.at[k],
            device_id=device, device_id_type=MESH,
        )

    def phi_row(x, carry):
        load(0, x).wait()
        total = gin[0, x]
        for c in range(1, 19):
            total = total + gin[c, x]
        ph[x + 1] = total
        yps[0, pl.ds(x, 1), :] = total[QY - 1 : QY]
        yps[1, pl.ds(x, 1), :] = total[0:1]
        return carry

    phi_row(0, 0)
    phi_row(QX - 1, 0)
    flat_x, plane_x = 7 - 7 * odd, 7 * odd
    main_slot = 1 - odd
    phi_copies = [
        remote(0, ph.at[flat_x + 1], ph.at[9 * odd], (flat_gx, gy)),
        remote(1, ph.at[plane_x + 1], wp.at[main_slot], (plane_gx, main_gy)),
        remote(2, ph.at[plane_x + 1], wp.at[1 - main_slot], (plane_gx, extra_gy)),
        remote(3, yps.at[0], yp.at[0], (gx, north)),
        remote(4, yps.at[1], yp.at[1], (gx, south)),
    ]
    pl.semaphore_wait(barrier, len(partners))
    for copy in (phi_copies[1], phi_copies[2], phi_copies[0]):
        copy.start()
    lax.fori_loop(1, QX - 1, phi_row, 0)
    for copy in phi_copies[3:]:
        copy.start()

    load_offsets.wait()
    plane = lax.rem((gx + odd) // 2, 4)
    fraction = (2 * plane + 1).astype(jnp.float32) * 0.125
    near = jnp.where(is_odd, fraction, 1.0 - fraction)
    far = 1.0 - near
    rest = off_ref[plane] - 8 * QY
    first = jnp.where(is_odd, QY - 1 - rest, rest)

    def interpolated(window, start):
        count = window.shape[0]
        here = pltpu.roll(window, lax.rem(count - start, count), 0)
        return near * here[:QY] + far * pltpu.roll(here, count - 1, 0)[:QY]

    row_y = lax.broadcasted_iota(jnp.int32, (QY, QZ), 0)

    def gradients(x):
        centre, minus, plus = ph[x + 1], ph[x], ph[x + 2]
        south_v = jnp.where(row_y == 0, yp[0, pl.ds(x, 1), :], pltpu.roll(centre, 1, 0))
        north_v = jnp.where(row_y == QY - 1, yp[1, pl.ds(x, 1), :], pltpu.roll(centre, QY - 1, 0))
        upper, lower = pltpu.roll(centre, QZ - 1, 1), pltpu.roll(centre, 1, 1)
        lap = (plus + minus) + (north_v + south_v) + (upper + lower) - 6.0 * centre
        mu = centre * (0.0625 * centre * centre - 0.0625) - 0.04 * lap
        half = 0.5 * mu
        mm[0] = mu
        mm[1] = half * (plus - minus)
        mm[2] = half * (north_v - south_v)
        mm[3] = half * (upper - lower)

    def collide_row(x, face):
        gradients(x)
        if face is not None:
            top = odd == face
            sign = jnp.where(top, 1.0, -1.0)
            jump = sign * (-plane_speed)

        def chunk(step, carry):
            zs = pl.ds(pl.multiple_of(step * 128, 128), 128)
            for h in range(2):
                rows = pl.ds(8 * h, 8)
                read = lambda ref, c: ref[c, x, rows, zs]
                f = [read(fin, c) for c in range(19)]
                phi = ph[x + 1, rows, zs]
                mu = mm[0, rows, zs]
                force = [mm[a, rows, zs] for a in (1, 2, 3)]
                diff = {c: f[c] - f[c + 1] for c in pairs}
                rho = f[0]
                for c in pairs:
                    rho = rho + (f[c] + f[c + 1])
                inverse = 1.0 / rho
                velocity = []
                for a in range(3):
                    total = 0.5 * force[a]
                    for c in pairs:
                        s = lattice_velocity[c][a]
                        if s:
                            total = total + diff[c] if s > 0 else total - diff[c]
                    velocity.append(total * inverse)
                ux, uy, uz = velocity
                u2 = ux * ux + uy * uy + uz * uz
                uf = ux * force[0] + uy * force[1] + uz * force[2]
                base = 1.25 * rho * (1.0 - 1.5 * u2) - 1.125 * uf
                scale = 5.625 * rho
                pull = [3.375 * part for part in force]
                gbase = (10.0 / 9.0) * (3.0 * mu - 1.5 * phi * u2)
                gscale = 5.0 * phi
                fin[0, x, rows, zs] = (1.0 / 3.0) * base - 0.25 * f[0]
                gin[0, x, rows, zs] = (10.0 / 9.0) * (phi - 2.0 * mu - 0.5 * phi * u2) - (
                    1.0 / 9.0
                ) * read(gin, 0)
                if face == 1:
                    common = -3.0 * uy - 1.5 * jump
                    wrho, wphi = jump * rho, jump * phi
                for c in pairs:
                    w = 1.0 / 18.0 if c < 7 else 1.0 / 36.0
                    direction = lattice_velocity[c]
                    p = axis_sum(direction, velocity)
                    b = axis_sum(direction, pull)
                    a = scale * p
                    ab = a + b
                    even = w * (base + p * ab)
                    oddpart = (w / 3.0) * (a + ab)
                    f_up = (even + oddpart) - 0.25 * f[c]
                    f_down = (even - oddpart) - 0.25 * f[c + 1]
                    h_p = gscale * p
                    geven = w * (gbase + p * h_p)
                    godd = (2.0 * w / 3.0) * h_p
                    g_up = (geven + godd) - (1.0 / 9.0) * read(gin, c)
                    g_down = (geven - godd) - (1.0 / 9.0) * read(gin, c + 1)
                    fin[c, x, rows, zs] = f_up
                    fin[c + 1, x, rows, zs] = f_down
                    gin[c, x, rows, zs] = g_up
                    gin[c + 1, x, rows, zs] = g_down
                    if face is not None and c in rising:
                        j = rising.index(c)
                        f_sent = jnp.where(top, f_up, f_down)
                        g_sent = jnp.where(top, g_up, g_down)
                        if face == 1:
                            cy = float(direction[1])
                            delta = common
                            if cy:
                                delta = delta + (cy * 9.0 * p + (cy * 3.0 * sign + 4.5 * jump))
                            f_sent = f_sent + w * (wrho * delta)
                            g_sent = g_sent + w * (wphi * delta)
                        sb[face, j, rows, zs] = f_sent
                        sb[face, 5 + j, rows, zs] = g_sent
            return carry

        lax.fori_loop(0, QZ // 128, chunk, 0)
        slot = jnp.where(top, 1, 0) if face is not None else x + 1
        group, line = slot // 4, lax.rem(slot, 4) * 10
        for d, chosen, y in ((0, northward, QY - 1), (1, southward, 0)):
            for j, c in enumerate(chosen):
                ys[d, group, pl.ds(line + j, 1), :] = fin[c, x, y : y + 1, :]
                ys[d, group, pl.ds(line + 5 + j, 1), :] = gin[c, x, y : y + 1, :]
        if face is not None:
            j_hi = jnp.where(top, 1, 2)
            for family in range(2):
                ce[face, 0, family : family + 1, :] = sb[face, j_hi + 5 * family, QY - 1 : QY, :]
                ce[face, 1, family : family + 1, :] = sb[face, 3 - j_hi + 5 * family, 0:1, :]

    def wait_f(x, carry):
        load(1, x).wait()
        return carry

    lax.fori_loop(0, QX, wait_f, 0)

    for copy in (phi_copies[0], phi_copies[3], phi_copies[4]):
        copy.wait_recv()
    collide_row(flat_x, 0)
    flat_copies = [
        remote(5, sb.at[0, pl.ds(0, 4)], ob.at[pl.ds(0, 4)], (flat_gx, gy)),
        remote(6, ce.at[0, 0], oc.at[0], (flat_gx, north)),
        remote(7, ce.at[0, 1], oc.at[1], (flat_gx, south)),
    ]
    for copy in flat_copies:
        copy.start()
    phi_copies[1].wait_recv()
    phi_copies[2].wait_recv()
    ph[9 * odd] = interpolated(wp[...].reshape(2 * QY, QZ), first)
    collide_row(plane_x, 1)
    plane_copies = [
        remote(8, ce.at[1, 0], we.at[0], (plane_gx, to_hi)),
        remote(9, ce.at[1, 1], we.at[1], (plane_gx, to_lo)),
    ]
    rows_at = lambda half, slot: wb.at[pl.ds(5 * half, 5), pl.ds(8 + QY * slot, QY)]
    layer = lambda half: sb.at[1, pl.ds(5 * half, 5)]
    main_copies = [
        remote(10 + half, layer(half), rows_at(half, main_slot), (plane_gx, main_gy))
        for half in range(2)
    ]
    extra_copies = [
        remote(16 + half, layer(half), rows_at(half, 1 - main_slot), (plane_gx, extra_gy))
        for half in range(2)
    ]
    hand_on = [
        pltpu.make_async_remote_copy(
            src_ref=rows_at(half, odd), dst_ref=rows_at(half, 1 - odd),
            send_sem=send_sem.at[19 + half], recv_sem=recv_sem.at[16 + half],
            device_id=(gx, core_gy), device_id_type=MESH,
        )
        for half in range(2)
    ]
    for copy in plane_copies + main_copies:
        copy.start()

    @pl.when(sends_twice)
    def _():
        for copy in extra_copies:
            copy.start()

    def inner_row(x, carry):
        collide_row(x, None)
        return carry

    side_copies = [
        remote(12 + 2 * d + group, ys.at[d, group], yr.at[d, group], (gx, (north, south)[d]))
        for group in range(2)
        for d in range(2)
    ]
    lax.fori_loop(1, 3, inner_row, 0)
    side_copies[0].start()
    side_copies[1].start()
    lax.fori_loop(3, QX - 1, inner_row, 0)
    side_copies[2].start()
    side_copies[3].start()

    families = ((fin, fo), (gin, go))

    def stream_level(x, carry):
        for source, target in families:
            for c in level:
                target[c, x] = streamed(source[c, x], *lattice_velocity[c][1:])
        return carry

    def stream_across(x, carry):
        for source, target in families:
            for c in rising:
                _, step_y, step_z = lattice_velocity[c]
                target[c, x + 1] = streamed(source[c, x], step_y, step_z)
                target[c + 1, x] = streamed(source[c + 1, x + 1], -step_y, -step_z)
        return carry

    lax.fori_loop(0, QX, stream_level, 0)
    flat_copies.append(remote(18, sb.at[0, pl.ds(4, 6)], ob.at[pl.ds(4, 6)], (flat_gx, gy)))
    flat_copies[-1].start()
    lax.fori_loop(0, QX - 1, stream_across, 0)

    for copy in side_copies:
        copy.wait_recv()

    def side_line(x):
        slot = jnp.where(x == 0, 0, jnp.where(x == QX - 1, 1, x + 1))
        return slot // 4, lax.rem(slot, 4) * 10

    def side_rows(x, chosen_x, shift):
        group, line = side_line(x)
        for d, chosen, y in ((0, northward, 0), (1, southward, QY - 1)):
            for j, c in enumerate(chosen):
                step_x, _, step_z = lattice_velocity[c]
                if step_x != chosen_x:
                    continue
                for family in range(2):
                    row = yr[d, group, pl.ds(line + 5 * family + j, 1), :]
                    if step_z:
                        row = pltpu.roll(row, step_z % QZ, 1)
                    families[family][1][c, x + shift, y : y + 1, :] = row

    def side_level(x, carry):
        side_rows(x, 0, 0)
        return carry

    def side_across(x, carry):
        side_rows(x, 1, 1)
        side_rows(x + 1, -1, -1)
        return carry

    lax.fori_loop(0, QX, side_level, 0)
    lax.fori_loop(0, QX - 1, side_across, 0)

    for copy in flat_copies:
        copy.wait_recv()

    def arrive_flat(sign, x):
        for j, c in enumerate(rising):
            step_y, step_z = sign * lattice_velocity[c][1], sign * lattice_velocity[c][2]
            c = c if sign > 0 else c + 1
            for family in range(2):
                v = streamed(ob[5 * family + j], step_y, step_z)
                if step_y > 0:
                    v = jnp.where(row_y == 0, oc[0, family : family + 1, :], v)
                elif step_y < 0:
                    v = jnp.where(row_y == QY - 1, oc[1, family : family + 1, :], v)
                families[family][1][c, x] = v

    pl.when(is_odd)(lambda: arrive_flat(1, 0))
    pl.when(jnp.logical_not(is_odd))(lambda: arrive_flat(-1, QX - 1))

    for half in range(2):
        main_copies[half].wait_recv()
        pl.when(sends_twice)(hand_on[half].start)
    for copy in plane_copies + extra_copies:
        copy.wait_recv()

    def arrive_plane(sign, x):
        for j, c in enumerate(rising):
            step_y, step_z = sign * lattice_velocity[c][1], sign * lattice_velocity[c][2]
            c = c if sign > 0 else c + 1
            for family in range(2):
                k = 5 * family + j
                if step_y > 0:
                    wb[k, 7:8, :] = we[0, family : family + 1, :]
                elif step_y < 0:
                    wb[k, 8 + 2 * QY : 9 + 2 * QY, :] = we[1, family : family + 1, :]
                v = interpolated(wb[k], first + (8 - step_y))
                families[family][1][c, x] = streamed(v, 0, step_z)

    pl.when(jnp.logical_not(is_odd))(lambda: arrive_plane(1, 0))
    pl.when(is_odd)(lambda: arrive_plane(-1, QX - 1))

    for copy in phi_copies + flat_copies + plane_copies + main_copies + side_copies:
        copy.wait_send()

    @pl.when(sends_twice)
    def _():
        for copy in extra_copies + hand_on:
            copy.wait_send()


def write_kernel(f, g, f_hbm, g_hbm, sem):
    copies = [
        pltpu.make_async_copy(source.at[:, x], target.at[:, x], sem.at[which, x])
        for x in range(QX)
        for which, (source, target) in enumerate(((f, f_hbm), (g, g_hbm)))
    ]
    for copy in copies:
        copy.start()
    for copy in copies:
        copy.wait()


def on_device(momentum_dist, order_dist, offsets):
    block = (19, QX, QY, QZ)
    f32 = jnp.float32
    vmem, hbm = pl.BlockSpec(memory_space=pltpu.VMEM), pl.BlockSpec(memory_space=pltpu.HBM)
    f_new, g_new = pl.pallas_call(
        step_kernel,
        out_shape=(pltpu.VMEM(block, f32), pltpu.VMEM(block, f32)),
        in_specs=[hbm, hbm, hbm],
        out_specs=(vmem, vmem),
        scratch_shapes=[
            pltpu.SMEM((4,), jnp.int32),
            pltpu.VMEM(block, f32),
            pltpu.VMEM(block, f32),
            pltpu.VMEM((QX + 2, QY, QZ), f32),
            pltpu.VMEM((2, QY, QZ), f32),
            pltpu.VMEM((2, QX, QZ), f32),
            pltpu.VMEM((2, QX, QZ), f32),
            pltpu.VMEM((4, QY, QZ), f32),
            pltpu.VMEM((2, 10, QY, QZ), f32),
            pltpu.VMEM((10, QY, QZ), f32),
            pltpu.VMEM((2, 2, QZ), f32),
            pltpu.VMEM((10, 2 * QY + 16, QZ), f32),
            pltpu.VMEM((2, 2, QZ), f32),
            pltpu.VMEM((2, 2, 2, QZ), f32),
            pltpu.VMEM((2, 2, 40, QZ), f32),
            pltpu.VMEM((2, 2, 40, QZ), f32),
            pltpu.SemaphoreType.DMA((2, QX)),
            pltpu.SemaphoreType.DMA,
            pltpu.SemaphoreType.DMA((21,)),
            pltpu.SemaphoreType.DMA((19,)),
        ],
        compiler_params=pltpu.CompilerParams(
            collective_id=0, has_side_effects=True, vmem_limit_bytes=32 * 2**20
        ),
    )(
        *(
            pltpu.with_memory_space_constraint(operand, pltpu.HBM)
            for operand in (offsets, momentum_dist, order_dist)
        )
    )
    whole = jax.ShapeDtypeStruct(block, f32)
    return pl.pallas_call(
        write_kernel,
        out_shape=(whole, whole),
        in_specs=[vmem, vmem],
        out_specs=(hbm, hbm),
        scratch_shapes=[pltpu.SemaphoreType.DMA((2, QX))],
        compiler_params=pltpu.CompilerParams(vmem_limit_bytes=4 * 2**20),
    )(
        pltpu.with_memory_space_constraint(f_new, pltpu.VMEM),
        pltpu.with_memory_space_constraint(g_new, pltpu.VMEM),
    )


def solution(mesh):
    return jax.shard_map(
        on_device,
        mesh=mesh,
        in_specs=(P(None, "gx", "gy", None), P(None, "gx", "gy", None), P()),
        out_specs=(P(None, "gx", "gy", None), P(None, "gx", "gy", None)),
        check_vma=False,
    )
```

```python
import jax
import jax.numpy as jnp
from jax import lax
from jax.experimental import pallas as pl
from jax.experimental.pallas import tpu as pltpu
from jax.sharding import PartitionSpec as P

lattice_velocity = [
    (0, 0, 0),
    (1, 0, 0),
    (-1, 0, 0),
    (0, 1, 0),
    (0, -1, 0),
    (0, 0, 1),
    (0, 0, -1),
    (1, 1, 0),
    (-1, -1, 0),
    (1, -1, 0),
    (-1, 1, 0),
    (1, 0, 1),
    (-1, 0, -1),
    (1, 0, -1),
    (-1, 0, 1),
    (0, 1, 1),
    (0, -1, -1),
    (0, 1, -1),
    (0, -1, 1),
]
plane_speed = 0.04
rising = [1, 7, 9, 11, 13]
northward = [3, 7, 10, 15, 17]
southward = [4, 8, 9, 16, 18]
level = [c for c in range(19) if lattice_velocity[c][0] == 0]
pairs = [1, 3, 5, 7, 9, 11, 13, 15, 17]
QX, QY, QZ = 8, 16, 512
NGX, NGY = 8, 16
MESH = pl.DeviceIdType.MESH


def axis_sum(direction, parts):
    total = None
    for sign, part in zip(direction, parts):
        if sign == 0:
            continue
        if total is None:
            total = part if sign > 0 else -part
        else:
            total = total + part if sign > 0 else total - part
    return total


def streamed(v, step_y, step_z):
    if step_z:
        v = pltpu.roll(v, step_z % QZ, 1)
    if step_y:
        v = pltpu.roll(v, step_y % QY, 0)
    return v


def step_kernel(
    off_hbm, f_hbm, g_hbm, fo, go,
    off_ref, fin, gin, ph, wp, yps, yp, mm, sb, ob, oc, wb, we, ce, ys, yr,
    load_sem, off_sem, send_sem, recv_sem,
):
    gx, gy = lax.axis_index("gx"), lax.axis_index("gy")
    odd = lax.rem(gx, 2)
    is_odd = odd == 1
    flat_gx = gx + 1 - 2 * odd
    plane_gx = lax.rem(gx + 2 * odd + NGX - 1, NGX)
    ring = lambda v: lax.rem(v + 2 * NGY, NGY)
    north, south = ring(gy + 1), ring(gy - 1)
    main_gy, extra_gy = ring(gy + 8), ring(gy + 9 - 18 * odd)
    core_gy = gy + 1 - 2 * lax.rem(gy, 2)
    sends_twice = lax.rem(gx + gy, 2) == 1
    to_hi, to_lo = ring(gy + 10 - 17 * odd), ring(gy + 7 - 17 * odd)
    partners = [
        (gx, north), (gx, south),
        (flat_gx, gy), (flat_gx, north), (flat_gx, south),
        (plane_gx, main_gy), (plane_gx, extra_gy), (plane_gx, to_hi), (plane_gx, to_lo),
    ]
    barrier = pltpu.get_barrier_semaphore()
    for partner in partners:
        pl.semaphore_signal(barrier, inc=1, device_id=partner, device_id_type=MESH)

    def load(which, x):
        source, target = ((g_hbm, gin), (f_hbm, fin))[which]
        return pltpu.make_async_copy(source.at[:, x], target.at[:, x], load_sem.at[which, x])

    for which in range(2):
        for x in (0, QX - 1, *range(1, QX - 1)):
            load(which, x).start()
    load_offsets = pltpu.make_async_copy(off_hbm, off_ref, off_sem)
    load_offsets.start()

    def remote(k, source, target, device):
        return pltpu.make_async_remote_copy(
            src_ref=source, dst_ref=target, send_sem=send_sem.at[k], recv_sem=recv_sem.at[k],
            device_id=device, device_id_type=MESH,
        )

    def phi_row(x, carry):
        load(0, x).wait()
        total = gin[0, x]
        for c in range(1, 19):
            total = total + gin[c, x]
        ph[x + 1] = total
        yps[0, pl.ds(x, 1), :] = total[QY - 1 : QY]
        yps[1, pl.ds(x, 1), :] = total[0:1]
        return carry

    phi_row(0, 0)
    phi_row(QX - 1, 0)
    flat_x, plane_x = 7 - 7 * odd, 7 * odd
    main_slot = 1 - odd
    phi_copies = [
        remote(0, ph.at[flat_x + 1], ph.at[9 * odd], (flat_gx, gy)),
        remote(1, ph.at[plane_x + 1], wp.at[main_slot], (plane_gx, main_gy)),
        remote(2, ph.at[plane_x + 1], wp.at[1 - main_slot], (plane_gx, extra_gy)),
        remote(3, yps.at[0], yp.at[0], (gx, north)),
        remote(4, yps.at[1], yp.at[1], (gx, south)),
    ]
    pl.semaphore_wait(barrier, len(partners))
    for copy in (phi_copies[1], phi_copies[2], phi_copies[0]):
        copy.start()
    lax.fori_loop(1, QX - 1, phi_row, 0)
    for copy in phi_copies[3:]:
        copy.start()

    load_offsets.wait()
    plane = lax.rem((gx + odd) // 2, 4)
    fraction = (2 * plane + 1).astype(jnp.float32) * 0.125
    near = jnp.where(is_odd, fraction, 1.0 - fraction)
    far = 1.0 - near
    rest = off_ref[plane] - 8 * QY
    first = jnp.where(is_odd, QY - 1 - rest, rest)

    def interpolated(window, start):
        count = window.shape[0]
        here = pltpu.roll(window, lax.rem(count - start, count), 0)
        return near * here[:QY] + far * pltpu.roll(here, count - 1, 0)[:QY]

    row_y = lax.broadcasted_iota(jnp.int32, (QY, QZ), 0)

    def gradients(x):
        centre, minus, plus = ph[x + 1], ph[x], ph[x + 2]
        south_v = jnp.where(row_y == 0, yp[0, pl.ds(x, 1), :], pltpu.roll(centre, 1, 0))
        north_v = jnp.where(row_y == QY - 1, yp[1, pl.ds(x, 1), :], pltpu.roll(centre, QY - 1, 0))
        upper, lower = pltpu.roll(centre, QZ - 1, 1), pltpu.roll(centre, 1, 1)
        lap = (plus + minus) + (north_v + south_v) + (upper + lower) - 6.0 * centre
        mu = centre * (0.0625 * centre * centre - 0.0625) - 0.04 * lap
        half = 0.5 * mu
        mm[0] = mu
        mm[1] = half * (plus - minus)
        mm[2] = half * (north_v - south_v)
        mm[3] = half * (upper - lower)

    def collide_row(x, face):
        gradients(x)
        if face is not None:
            top = odd == face
            sign = jnp.where(top, 1.0, -1.0)
            jump = sign * (-plane_speed)

        def chunk(step, carry):
            zs = pl.ds(pl.multiple_of(step * 128, 128), 128)
            for h in range(2):
                rows = pl.ds(8 * h, 8)
                read = lambda ref, c: ref[c, x, rows, zs]
                f = [read(fin, c) for c in range(19)]
                phi = ph[x + 1, rows, zs]
                mu = mm[0, rows, zs]
                force = [mm[a, rows, zs] for a in (1, 2, 3)]
                diff = {c: f[c] - f[c + 1] for c in pairs}
                rho = f[0]
                for c in pairs:
                    rho = rho + (f[c] + f[c + 1])
                inverse = 1.0 / rho
                velocity = []
                for a in range(3):
                    total = 0.5 * force[a]
                    for c in pairs:
                        s = lattice_velocity[c][a]
                        if s:
                            total = total + diff[c] if s > 0 else total - diff[c]
                    velocity.append(total * inverse)
                ux, uy, uz = velocity
                u2 = ux * ux + uy * uy + uz * uz
                uf = ux * force[0] + uy * force[1] + uz * force[2]
                base = 1.25 * rho * (1.0 - 1.5 * u2) - 1.125 * uf
                scale = 5.625 * rho
                pull = [3.375 * part for part in force]
                gbase = (10.0 / 9.0) * (3.0 * mu - 1.5 * phi * u2)
                gscale = 5.0 * phi
                fin[0, x, rows, zs] = (1.0 / 3.0) * base - 0.25 * f[0]
                gin[0, x, rows, zs] = (10.0 / 9.0) * (phi - 2.0 * mu - 0.5 * phi * u2) - (
                    1.0 / 9.0
                ) * read(gin, 0)
                if face == 1:
                    common = -3.0 * uy - 1.5 * jump
                    wrho, wphi = jump * rho, jump * phi
                for c in pairs:
                    w = 1.0 / 18.0 if c < 7 else 1.0 / 36.0
                    direction = lattice_velocity[c]
                    p = axis_sum(direction, velocity)
                    b = axis_sum(direction, pull)
                    a = scale * p
                    ab = a + b
                    even = w * (base + p * ab)
                    oddpart = (w / 3.0) * (a + ab)
                    f_up = (even + oddpart) - 0.25 * f[c]
                    f_down = (even - oddpart) - 0.25 * f[c + 1]
                    h_p = gscale * p
                    geven = w * (gbase + p * h_p)
                    godd = (2.0 * w / 3.0) * h_p
                    g_up = (geven + godd) - (1.0 / 9.0) * read(gin, c)
                    g_down = (geven - godd) - (1.0 / 9.0) * read(gin, c + 1)
                    fin[c, x, rows, zs] = f_up
                    fin[c + 1, x, rows, zs] = f_down
                    gin[c, x, rows, zs] = g_up
                    gin[c + 1, x, rows, zs] = g_down
                    if face is not None and c in rising:
                        j = rising.index(c)
                        f_sent = jnp.where(top, f_up, f_down)
                        g_sent = jnp.where(top, g_up, g_down)
                        if face == 1:
                            cy = float(direction[1])
                            delta = common
                            if cy:
                                delta = delta + (cy * 9.0 * p + (cy * 3.0 * sign + 4.5 * jump))
                            f_sent = f_sent + w * (wrho * delta)
                            g_sent = g_sent + w * (wphi * delta)
                        sb[face, j, rows, zs] = f_sent
                        sb[face, 5 + j, rows, zs] = g_sent
            return carry

        lax.fori_loop(0, QZ // 128, chunk, 0)
        slot = jnp.where(top, 1, 0) if face is not None else x + 1
        group, line = slot // 4, lax.rem(slot, 4) * 10
        for d, chosen, y in ((0, northward, QY - 1), (1, southward, 0)):
            for j, c in enumerate(chosen):
                ys[d, group, pl.ds(line + j, 1), :] = fin[c, x, y : y + 1, :]
                ys[d, group, pl.ds(line + 5 + j, 1), :] = gin[c, x, y : y + 1, :]
        if face is not None:
            j_hi = jnp.where(top, 1, 2)
            for family in range(2):
                ce[face, 0, family : family + 1, :] = sb[face, j_hi + 5 * family, QY - 1 : QY, :]
                ce[face, 1, family : family + 1, :] = sb[face, 3 - j_hi + 5 * family, 0:1, :]

    def wait_f(x, carry):
        load(1, x).wait()
        return carry

    lax.fori_loop(0, QX, wait_f, 0)

    for copy in (phi_copies[0], phi_copies[3], phi_copies[4]):
        copy.wait_recv()
    collide_row(flat_x, 0)
    flat_copies = [
        remote(5, sb.at[0, pl.ds(0, 4)], ob.at[pl.ds(0, 4)], (flat_gx, gy)),
        remote(6, ce.at[0, 0], oc.at[0], (flat_gx, north)),
        remote(7, ce.at[0, 1], oc.at[1], (flat_gx, south)),
    ]
    for copy in flat_copies:
        copy.start()
    phi_copies[1].wait_recv()
    phi_copies[2].wait_recv()
    ph[9 * odd] = interpolated(wp[...].reshape(2 * QY, QZ), first)
    collide_row(plane_x, 1)
    plane_copies = [
        remote(8, ce.at[1, 0], we.at[0], (plane_gx, to_hi)),
        remote(9, ce.at[1, 1], we.at[1], (plane_gx, to_lo)),
    ]
    rows_at = lambda half, slot: wb.at[pl.ds(5 * half, 5), pl.ds(8 + QY * slot, QY)]
    layer = lambda half: sb.at[1, pl.ds(5 * half, 5)]
    main_copies = [
        remote(10 + half, layer(half), rows_at(half, main_slot), (plane_gx, main_gy))
        for half in range(2)
    ]
    extra_copies = [
        remote(16 + half, layer(half), rows_at(half, 1 - main_slot), (plane_gx, extra_gy))
        for half in range(2)
    ]
    hand_on = [
        pltpu.make_async_remote_copy(
            src_ref=rows_at(half, odd), dst_ref=rows_at(half, 1 - odd),
            send_sem=send_sem.at[19 + half], recv_sem=recv_sem.at[16 + half],
            device_id=(gx, core_gy), device_id_type=MESH,
        )
        for half in range(2)
    ]
    for copy in plane_copies + main_copies:
        copy.start()

    @pl.when(sends_twice)
    def _():
        for copy in extra_copies:
            copy.start()

    def inner_row(x, carry):
        collide_row(x, None)
        return carry

    side_copies = [
        remote(12 + 2 * d + group, ys.at[d, group], yr.at[d, group], (gx, (north, south)[d]))
        for group in range(2)
        for d in range(2)
    ]
    lax.fori_loop(1, 3, inner_row, 0)
    side_copies[0].start()
    side_copies[1].start()
    lax.fori_loop(3, QX - 1, inner_row, 0)
    side_copies[2].start()
    side_copies[3].start()

    families = ((fin, fo), (gin, go))

    def stream_level(x, carry):
        for source, target in families:
            for c in level:
                target[c, x] = streamed(source[c, x], *lattice_velocity[c][1:])
        return carry

    def stream_across(x, carry):
        for source, target in families:
            for c in rising:
                _, step_y, step_z = lattice_velocity[c]
                target[c, x + 1] = streamed(source[c, x], step_y, step_z)
                target[c + 1, x] = streamed(source[c + 1, x + 1], -step_y, -step_z)
        return carry

    lax.fori_loop(0, QX, stream_level, 0)
    flat_copies.append(remote(18, sb.at[0, pl.ds(4, 6)], ob.at[pl.ds(4, 6)], (flat_gx, gy)))
    flat_copies[-1].start()
    lax.fori_loop(0, QX - 1, stream_across, 0)

    for copy in side_copies:
        copy.wait_recv()

    def side_line(x):
        slot = jnp.where(x == 0, 0, jnp.where(x == QX - 1, 1, x + 1))
        return slot // 4, lax.rem(slot, 4) * 10

    def side_rows(x, chosen_x, shift):
        group, line = side_line(x)
        for d, chosen, y in ((0, northward, 0), (1, southward, QY - 1)):
            for j, c in enumerate(chosen):
                step_x, _, step_z = lattice_velocity[c]
                if step_x != chosen_x:
                    continue
                for family in range(2):
                    row = yr[d, group, pl.ds(line + 5 * family + j, 1), :]
                    if step_z:
                        row = pltpu.roll(row, step_z % QZ, 1)
                    families[family][1][c, x + shift, y : y + 1, :] = row

    def side_level(x, carry):
        side_rows(x, 0, 0)
        return carry

    def side_across(x, carry):
        side_rows(x, 1, 1)
        side_rows(x + 1, -1, -1)
        return carry

    lax.fori_loop(0, QX, side_level, 0)
    lax.fori_loop(0, QX - 1, side_across, 0)

    for half in range(2):
        main_copies[half].wait_recv()
        pl.when(sends_twice)(hand_on[half].start)

    for copy in flat_copies:
        copy.wait_recv()

    def arrive_flat(sign, x):
        for j, c in enumerate(rising):
            step_y, step_z = sign * lattice_velocity[c][1], sign * lattice_velocity[c][2]
            c = c if sign > 0 else c + 1
            for family in range(2):
                v = streamed(ob[5 * family + j], step_y, step_z)
                if step_y > 0:
                    v = jnp.where(row_y == 0, oc[0, family : family + 1, :], v)
                elif step_y < 0:
                    v = jnp.where(row_y == QY - 1, oc[1, family : family + 1, :], v)
                families[family][1][c, x] = v

    pl.when(is_odd)(lambda: arrive_flat(1, 0))
    pl.when(jnp.logical_not(is_odd))(lambda: arrive_flat(-1, QX - 1))

    for copy in plane_copies + extra_copies:
        copy.wait_recv()

    def arrive_plane(sign, x):
        for j, c in enumerate(rising):
            step_y, step_z = sign * lattice_velocity[c][1], sign * lattice_velocity[c][2]
            c = c if sign > 0 else c + 1
            for family in range(2):
                k = 5 * family + j
                if step_y > 0:
                    wb[k, 7:8, :] = we[0, family : family + 1, :]
                elif step_y < 0:
                    wb[k, 8 + 2 * QY : 9 + 2 * QY, :] = we[1, family : family + 1, :]
                v = interpolated(wb[k], first + (8 - step_y))
                families[family][1][c, x] = streamed(v, 0, step_z)

    pl.when(jnp.logical_not(is_odd))(lambda: arrive_plane(1, 0))
    pl.when(is_odd)(lambda: arrive_plane(-1, QX - 1))

    for copy in phi_copies + flat_copies + plane_copies + main_copies + side_copies:
        copy.wait_send()

    @pl.when(sends_twice)
    def _():
        for copy in extra_copies + hand_on:
            copy.wait_send()


def write_kernel(f, g, f_hbm, g_hbm, sem):
    copies = [
        pltpu.make_async_copy(source.at[:, x], target.at[:, x], sem.at[which, x])
        for x in range(QX)
        for which, (source, target) in enumerate(((f, f_hbm), (g, g_hbm)))
    ]
    for copy in copies:
        copy.start()
    for copy in copies:
        copy.wait()


def on_device(momentum_dist, order_dist, offsets):
    block = (19, QX, QY, QZ)
    f32 = jnp.float32
    vmem, hbm = pl.BlockSpec(memory_space=pltpu.VMEM), pl.BlockSpec(memory_space=pltpu.HBM)
    f_new, g_new = pl.pallas_call(
        step_kernel,
        out_shape=(pltpu.VMEM(block, f32), pltpu.VMEM(block, f32)),
        in_specs=[hbm, hbm, hbm],
        out_specs=(vmem, vmem),
        scratch_shapes=[
            pltpu.SMEM((4,), jnp.int32),
            pltpu.VMEM(block, f32),
            pltpu.VMEM(block, f32),
            pltpu.VMEM((QX + 2, QY, QZ), f32),
            pltpu.VMEM((2, QY, QZ), f32),
            pltpu.VMEM((2, QX, QZ), f32),
            pltpu.VMEM((2, QX, QZ), f32),
            pltpu.VMEM((4, QY, QZ), f32),
            pltpu.VMEM((2, 10, QY, QZ), f32),
            pltpu.VMEM((10, QY, QZ), f32),
            pltpu.VMEM((2, 2, QZ), f32),
            pltpu.VMEM((10, 2 * QY + 16, QZ), f32),
            pltpu.VMEM((2, 2, QZ), f32),
            pltpu.VMEM((2, 2, 2, QZ), f32),
            pltpu.VMEM((2, 2, 40, QZ), f32),
            pltpu.VMEM((2, 2, 40, QZ), f32),
            pltpu.SemaphoreType.DMA((2, QX)),
            pltpu.SemaphoreType.DMA,
            pltpu.SemaphoreType.DMA((21,)),
            pltpu.SemaphoreType.DMA((19,)),
        ],
        compiler_params=pltpu.CompilerParams(
            collective_id=0, has_side_effects=True, vmem_limit_bytes=32 * 2**20
        ),
    )(
        *(
            pltpu.with_memory_space_constraint(operand, pltpu.HBM)
            for operand in (offsets, momentum_dist, order_dist)
        )
    )
    whole = jax.ShapeDtypeStruct(block, f32)
    return pl.pallas_call(
        write_kernel,
        out_shape=(whole, whole),
        in_specs=[vmem, vmem],
        out_specs=(hbm, hbm),
        scratch_shapes=[pltpu.SemaphoreType.DMA((2, QX))],
        compiler_params=pltpu.CompilerParams(vmem_limit_bytes=4 * 2**20),
    )(
        pltpu.with_memory_space_constraint(f_new, pltpu.VMEM),
        pltpu.with_memory_space_constraint(g_new, pltpu.VMEM),
    )


def solution(mesh):
    return jax.shard_map(
        on_device,
        mesh=mesh,
        in_specs=(P(None, "gx", "gy", None), P(None, "gx", "gy", None), P()),
        out_specs=(P(None, "gx", "gy", None), P(None, "gx", "gy", None)),
        check_vma=False,
    )
```

```python
import jax
import jax.numpy as jnp
from jax import lax
from jax.experimental import pallas as pl
from jax.experimental.pallas import tpu as pltpu
from jax.sharding import PartitionSpec as P

lattice_velocity = [
    (0, 0, 0),
    (1, 0, 0),
    (-1, 0, 0),
    (0, 1, 0),
    (0, -1, 0),
    (0, 0, 1),
    (0, 0, -1),
    (1, 1, 0),
    (-1, -1, 0),
    (1, -1, 0),
    (-1, 1, 0),
    (1, 0, 1),
    (-1, 0, -1),
    (1, 0, -1),
    (-1, 0, 1),
    (0, 1, 1),
    (0, -1, -1),
    (0, 1, -1),
    (0, -1, 1),
]
plane_speed = 0.04
rising = [1, 7, 9, 11, 13]
northward = [3, 7, 10, 15, 17]
southward = [4, 8, 9, 16, 18]
level = [c for c in range(19) if lattice_velocity[c][0] == 0]
pairs = [1, 3, 5, 7, 9, 11, 13, 15, 17]
QX, QY, QZ = 8, 16, 512
NGX, NGY = 8, 16
MESH = pl.DeviceIdType.MESH


def axis_sum(direction, parts):
    total = None
    for sign, part in zip(direction, parts):
        if sign == 0:
            continue
        if total is None:
            total = part if sign > 0 else -part
        else:
            total = total + part if sign > 0 else total - part
    return total


def streamed(v, step_y, step_z):
    if step_z:
        v = pltpu.roll(v, step_z % QZ, 1)
    if step_y:
        v = pltpu.roll(v, step_y % QY, 0)
    return v


def step_kernel(
    off_hbm, f_hbm, g_hbm, fo, go,
    off_ref, fin, gin, ph, wp, yps, yp, mm, sb, ob, oc, wb, we, ce, ys, yr,
    load_sem, off_sem, send_sem, recv_sem,
):
    gx, gy = lax.axis_index("gx"), lax.axis_index("gy")
    odd = lax.rem(gx, 2)
    is_odd = odd == 1
    flat_gx = gx + 1 - 2 * odd
    plane_gx = lax.rem(gx + 2 * odd + NGX - 1, NGX)
    ring = lambda v: lax.rem(v + 2 * NGY, NGY)
    north, south = ring(gy + 1), ring(gy - 1)
    main_gy, extra_gy = ring(gy + 8), ring(gy + 9 - 18 * odd)
    core_gy = gy + 1 - 2 * lax.rem(gy, 2)
    sends_twice = lax.rem(gx + gy, 2) == 1
    to_hi, to_lo = ring(gy + 10 - 17 * odd), ring(gy + 7 - 17 * odd)
    partners = [
        (gx, north), (gx, south),
        (flat_gx, gy), (flat_gx, north), (flat_gx, south),
        (plane_gx, main_gy), (plane_gx, extra_gy), (plane_gx, to_hi), (plane_gx, to_lo),
    ]
    barrier = pltpu.get_barrier_semaphore()
    for partner in partners:
        pl.semaphore_signal(barrier, inc=1, device_id=partner, device_id_type=MESH)

    def load(which, x):
        source, target = ((g_hbm, gin), (f_hbm, fin))[which]
        return pltpu.make_async_copy(source.at[:, x], target.at[:, x], load_sem.at[which, x])

    for which in range(2):
        for x in (0, QX - 1, *range(1, QX - 1)):
            load(which, x).start()
    load_offsets = pltpu.make_async_copy(off_hbm, off_ref, off_sem)
    load_offsets.start()

    def remote(k, source, target, device):
        return pltpu.make_async_remote_copy(
            src_ref=source, dst_ref=target, send_sem=send_sem.at[k], recv_sem=recv_sem.at[k],
            device_id=device, device_id_type=MESH,
        )

    def phi_row(x, carry):
        load(0, x).wait()
        total = gin[0, x]
        for c in range(1, 19):
            total = total + gin[c, x]
        ph[x + 1] = total
        yps[0, pl.ds(x, 1), :] = total[QY - 1 : QY]
        yps[1, pl.ds(x, 1), :] = total[0:1]
        return carry

    phi_row(0, 0)
    phi_row(QX - 1, 0)
    flat_x, plane_x = 7 - 7 * odd, 7 * odd
    main_slot = 1 - odd
    phi_copies = [
        remote(0, ph.at[flat_x + 1], ph.at[9 * odd], (flat_gx, gy)),
        remote(1, ph.at[plane_x + 1], wp.at[main_slot], (plane_gx, main_gy)),
        remote(2, ph.at[plane_x + 1], wp.at[1 - main_slot], (plane_gx, extra_gy)),
        remote(3, yps.at[0], yp.at[0], (gx, north)),
        remote(4, yps.at[1], yp.at[1], (gx, south)),
    ]
    pl.semaphore_wait(barrier, len(partners))
    for copy in (phi_copies[1], phi_copies[2], phi_copies[0]):
        copy.start()
    lax.fori_loop(1, QX - 1, phi_row, 0)
    for copy in phi_copies[3:]:
        copy.start()

    load_offsets.wait()
    plane = lax.rem((gx + odd) // 2, 4)
    fraction = (2 * plane + 1).astype(jnp.float32) * 0.125
    near = jnp.where(is_odd, fraction, 1.0 - fraction)
    far = 1.0 - near
    rest = off_ref[plane] - 8 * QY
    first = jnp.where(is_odd, QY - 1 - rest, rest)

    def interpolated(window, start):
        count = window.shape[0]
        here = pltpu.roll(window, lax.rem(count - start, count), 0)
        return near * here[:QY] + far * pltpu.roll(here, count - 1, 0)[:QY]

    row_y = lax.broadcasted_iota(jnp.int32, (QY, QZ), 0)

    def gradients(x):
        centre, minus, plus = ph[x + 1], ph[x], ph[x + 2]
        south_v = jnp.where(row_y == 0, yp[0, pl.ds(x, 1), :], pltpu.roll(centre, 1, 0))
        north_v = jnp.where(row_y == QY - 1, yp[1, pl.ds(x, 1), :], pltpu.roll(centre, QY - 1, 0))
        upper, lower = pltpu.roll(centre, QZ - 1, 1), pltpu.roll(centre, 1, 1)
        lap = (plus + minus) + (north_v + south_v) + (upper + lower) - 6.0 * centre
        mu = centre * (0.0625 * centre * centre - 0.0625) - 0.04 * lap
        half = 0.5 * mu
        mm[0] = mu
        mm[1] = half * (plus - minus)
        mm[2] = half * (north_v - south_v)
        mm[3] = half * (upper - lower)

    def collide_row(x, face):
        gradients(x)
        if face is not None:
            top = odd == face
            sign = jnp.where(top, 1.0, -1.0)
            jump = sign * (-plane_speed)

        def chunk(step, carry):
            zs = pl.ds(pl.multiple_of(step * 128, 128), 128)
            for h in range(2):
                rows = pl.ds(8 * h, 8)
                read = lambda ref, c: ref[c, x, rows, zs]
                f = [read(fin, c) for c in range(19)]
                phi = ph[x + 1, rows, zs]
                mu = mm[0, rows, zs]
                force = [mm[a, rows, zs] for a in (1, 2, 3)]
                diff = {c: f[c] - f[c + 1] for c in pairs}
                rho = f[0]
                for c in pairs:
                    rho = rho + (f[c] + f[c + 1])
                inverse = 1.0 / rho
                velocity = []
                for a in range(3):
                    total = 0.5 * force[a]
                    for c in pairs:
                        s = lattice_velocity[c][a]
                        if s:
                            total = total + diff[c] if s > 0 else total - diff[c]
                    velocity.append(total * inverse)
                ux, uy, uz = velocity
                u2 = ux * ux + uy * uy + uz * uz
                uf = ux * force[0] + uy * force[1] + uz * force[2]
                base = 1.25 * rho * (1.0 - 1.5 * u2) - 1.125 * uf
                scale = 5.625 * rho
                pull = [3.375 * part for part in force]
                gbase = (10.0 / 9.0) * (3.0 * mu - 1.5 * phi * u2)
                gscale = 5.0 * phi
                fin[0, x, rows, zs] = (1.0 / 3.0) * base - 0.25 * f[0]
                gin[0, x, rows, zs] = (10.0 / 9.0) * (phi - 2.0 * mu - 0.5 * phi * u2) - (
                    1.0 / 9.0
                ) * read(gin, 0)
                if face == 1:
                    common = -3.0 * uy - 1.5 * jump
                    wrho, wphi = jump * rho, jump * phi
                for c in pairs:
                    w = 1.0 / 18.0 if c < 7 else 1.0 / 36.0
                    direction = lattice_velocity[c]
                    p = axis_sum(direction, velocity)
                    b = axis_sum(direction, pull)
                    a = scale * p
                    ab = a + b
                    even = w * (base + p * ab)
                    oddpart = (w / 3.0) * (a + ab)
                    f_up = (even + oddpart) - 0.25 * f[c]
                    f_down = (even - oddpart) - 0.25 * f[c + 1]
                    h_p = gscale * p
                    geven = w * (gbase + p * h_p)
                    godd = (2.0 * w / 3.0) * h_p
                    g_up = (geven + godd) - (1.0 / 9.0) * read(gin, c)
                    g_down = (geven - godd) - (1.0 / 9.0) * read(gin, c + 1)
                    fin[c, x, rows, zs] = f_up
                    fin[c + 1, x, rows, zs] = f_down
                    gin[c, x, rows, zs] = g_up
                    gin[c + 1, x, rows, zs] = g_down
                    if face is not None and c in rising:
                        j = rising.index(c)
                        f_sent = jnp.where(top, f_up, f_down)
                        g_sent = jnp.where(top, g_up, g_down)
                        if face == 1:
                            cy = float(direction[1])
                            delta = common
                            if cy:
                                delta = delta + (cy * 9.0 * p + (cy * 3.0 * sign + 4.5 * jump))
                            f_sent = f_sent + w * (wrho * delta)
                            g_sent = g_sent + w * (wphi * delta)
                        sb[face, j, rows, zs] = f_sent
                        sb[face, 5 + j, rows, zs] = g_sent
            return carry

        lax.fori_loop(0, QZ // 128, chunk, 0)
        slot = jnp.where(top, 1, 0) if face is not None else x + 1
        group, line = slot // 4, lax.rem(slot, 4) * 10
        for d, chosen, y in ((0, northward, QY - 1), (1, southward, 0)):
            for j, c in enumerate(chosen):
                ys[d, group, pl.ds(line + j, 1), :] = fin[c, x, y : y + 1, :]
                ys[d, group, pl.ds(line + 5 + j, 1), :] = gin[c, x, y : y + 1, :]
        if face is not None:
            j_hi = jnp.where(top, 1, 2)
            for family in range(2):
                ce[face, 0, family : family + 1, :] = sb[face, j_hi + 5 * family, QY - 1 : QY, :]
                ce[face, 1, family : family + 1, :] = sb[face, 3 - j_hi + 5 * family, 0:1, :]

    def wait_f(x, carry):
        load(1, x).wait()
        return carry

    lax.fori_loop(0, QX, wait_f, 0)

    for copy in (phi_copies[0], phi_copies[3], phi_copies[4]):
        copy.wait_recv()
    collide_row(flat_x, 0)
    flat_copies = [
        remote(5, sb.at[0, pl.ds(0, 4)], ob.at[pl.ds(0, 4)], (flat_gx, gy)),
        remote(6, ce.at[0, 0], oc.at[0], (flat_gx, north)),
        remote(7, ce.at[0, 1], oc.at[1], (flat_gx, south)),
    ]
    for copy in flat_copies:
        copy.start()
    def inner_row(x, carry):
        collide_row(x, None)
        return carry

    lax.fori_loop(1, 3, inner_row, 0)
    phi_copies[1].wait_recv()
    phi_copies[2].wait_recv()
    ph[9 * odd] = interpolated(wp[...].reshape(2 * QY, QZ), first)
    collide_row(plane_x, 1)
    plane_copies = [
        remote(8, ce.at[1, 0], we.at[0], (plane_gx, to_hi)),
        remote(9, ce.at[1, 1], we.at[1], (plane_gx, to_lo)),
    ]
    rows_at = lambda half, slot: wb.at[pl.ds(5 * half, 5), pl.ds(8 + QY * slot, QY)]
    layer = lambda half: sb.at[1, pl.ds(5 * half, 5)]
    main_copies = [
        remote(10 + half, layer(half), rows_at(half, main_slot), (plane_gx, main_gy))
        for half in range(2)
    ]
    extra_copies = [
        remote(16 + half, layer(half), rows_at(half, 1 - main_slot), (plane_gx, extra_gy))
        for half in range(2)
    ]
    hand_on = [
        pltpu.make_async_remote_copy(
            src_ref=rows_at(half, odd), dst_ref=rows_at(half, 1 - odd),
            send_sem=send_sem.at[19 + half], recv_sem=recv_sem.at[16 + half],
            device_id=(gx, core_gy), device_id_type=MESH,
        )
        for half in range(2)
    ]
    for copy in plane_copies + main_copies:
        copy.start()

    @pl.when(sends_twice)
    def _():
        for copy in extra_copies:
            copy.start()

    side_copies = [
        remote(12 + 2 * d + group, ys.at[d, group], yr.at[d, group], (gx, (north, south)[d]))
        for group in range(2)
        for d in range(2)
    ]
    side_copies[0].start()
    side_copies[1].start()
    lax.fori_loop(3, QX - 1, inner_row, 0)
    side_copies[2].start()
    side_copies[3].start()

    families = ((fin, fo), (gin, go))

    def stream_level(x, carry):
        for source, target in families:
            for c in level:
                target[c, x] = streamed(source[c, x], *lattice_velocity[c][1:])
        return carry

    def stream_across(x, carry):
        for source, target in families:
            for c in rising:
                _, step_y, step_z = lattice_velocity[c]
                target[c, x + 1] = streamed(source[c, x], step_y, step_z)
                target[c + 1, x] = streamed(source[c + 1, x + 1], -step_y, -step_z)
        return carry

    lax.fori_loop(0, QX, stream_level, 0)
    flat_copies.append(remote(18, sb.at[0, pl.ds(4, 6)], ob.at[pl.ds(4, 6)], (flat_gx, gy)))
    flat_copies[-1].start()
    lax.fori_loop(0, QX - 1, stream_across, 0)

    for copy in side_copies:
        copy.wait_recv()

    def side_line(x):
        slot = jnp.where(x == 0, 0, jnp.where(x == QX - 1, 1, x + 1))
        return slot // 4, lax.rem(slot, 4) * 10

    def side_rows(x, chosen_x, shift):
        group, line = side_line(x)
        for d, chosen, y in ((0, northward, 0), (1, southward, QY - 1)):
            for j, c in enumerate(chosen):
                step_x, _, step_z = lattice_velocity[c]
                if step_x != chosen_x:
                    continue
                for family in range(2):
                    row = yr[d, group, pl.ds(line + 5 * family + j, 1), :]
                    if step_z:
                        row = pltpu.roll(row, step_z % QZ, 1)
                    families[family][1][c, x + shift, y : y + 1, :] = row

    def side_level(x, carry):
        side_rows(x, 0, 0)
        return carry

    def side_across(x, carry):
        side_rows(x, 1, 1)
        side_rows(x + 1, -1, -1)
        return carry

    lax.fori_loop(0, QX, side_level, 0)
    lax.fori_loop(0, QX - 1, side_across, 0)

    for half in range(2):
        main_copies[half].wait_recv()
        pl.when(sends_twice)(hand_on[half].start)

    for copy in flat_copies:
        copy.wait_recv()

    def arrive_flat(sign, x):
        for j, c in enumerate(rising):
            step_y, step_z = sign * lattice_velocity[c][1], sign * lattice_velocity[c][2]
            c = c if sign > 0 else c + 1
            for family in range(2):
                v = streamed(ob[5 * family + j], step_y, step_z)
                if step_y > 0:
                    v = jnp.where(row_y == 0, oc[0, family : family + 1, :], v)
                elif step_y < 0:
                    v = jnp.where(row_y == QY - 1, oc[1, family : family + 1, :], v)
                families[family][1][c, x] = v

    pl.when(is_odd)(lambda: arrive_flat(1, 0))
    pl.when(jnp.logical_not(is_odd))(lambda: arrive_flat(-1, QX - 1))

    for copy in plane_copies + extra_copies:
        copy.wait_recv()

    def arrive_plane(sign, x):
        for j, c in enumerate(rising):
            step_y, step_z = sign * lattice_velocity[c][1], sign * lattice_velocity[c][2]
            c = c if sign > 0 else c + 1
            for family in range(2):
                k = 5 * family + j
                if step_y > 0:
                    wb[k, 7:8, :] = we[0, family : family + 1, :]
                elif step_y < 0:
                    wb[k, 8 + 2 * QY : 9 + 2 * QY, :] = we[1, family : family + 1, :]
                v = interpolated(wb[k], first + (8 - step_y))
                families[family][1][c, x] = streamed(v, 0, step_z)

    pl.when(jnp.logical_not(is_odd))(lambda: arrive_plane(1, 0))
    pl.when(is_odd)(lambda: arrive_plane(-1, QX - 1))

    for copy in phi_copies + flat_copies + plane_copies + main_copies + side_copies:
        copy.wait_send()

    @pl.when(sends_twice)
    def _():
        for copy in extra_copies + hand_on:
            copy.wait_send()


def write_kernel(f, g, f_hbm, g_hbm, sem):
    copies = [
        pltpu.make_async_copy(source.at[:, x], target.at[:, x], sem.at[which, x])
        for x in range(QX)
        for which, (source, target) in enumerate(((f, f_hbm), (g, g_hbm)))
    ]
    for copy in copies:
        copy.start()
    for copy in copies:
        copy.wait()


def on_device(momentum_dist, order_dist, offsets):
    block = (19, QX, QY, QZ)
    f32 = jnp.float32
    vmem, hbm = pl.BlockSpec(memory_space=pltpu.VMEM), pl.BlockSpec(memory_space=pltpu.HBM)
    f_new, g_new = pl.pallas_call(
        step_kernel,
        out_shape=(pltpu.VMEM(block, f32), pltpu.VMEM(block, f32)),
        in_specs=[hbm, hbm, hbm],
        out_specs=(vmem, vmem),
        scratch_shapes=[
            pltpu.SMEM((4,), jnp.int32),
            pltpu.VMEM(block, f32),
            pltpu.VMEM(block, f32),
            pltpu.VMEM((QX + 2, QY, QZ), f32),
            pltpu.VMEM((2, QY, QZ), f32),
            pltpu.VMEM((2, QX, QZ), f32),
            pltpu.VMEM((2, QX, QZ), f32),
            pltpu.VMEM((4, QY, QZ), f32),
            pltpu.VMEM((2, 10, QY, QZ), f32),
            pltpu.VMEM((10, QY, QZ), f32),
            pltpu.VMEM((2, 2, QZ), f32),
            pltpu.VMEM((10, 2 * QY + 16, QZ), f32),
            pltpu.VMEM((2, 2, QZ), f32),
            pltpu.VMEM((2, 2, 2, QZ), f32),
            pltpu.VMEM((2, 2, 40, QZ), f32),
            pltpu.VMEM((2, 2, 40, QZ), f32),
            pltpu.SemaphoreType.DMA((2, QX)),
            pltpu.SemaphoreType.DMA,
            pltpu.SemaphoreType.DMA((21,)),
            pltpu.SemaphoreType.DMA((19,)),
        ],
        compiler_params=pltpu.CompilerParams(
            collective_id=0, has_side_effects=True, vmem_limit_bytes=32 * 2**20
        ),
    )(
        *(
            pltpu.with_memory_space_constraint(operand, pltpu.HBM)
            for operand in (offsets, momentum_dist, order_dist)
        )
    )
    whole = jax.ShapeDtypeStruct(block, f32)
    return pl.pallas_call(
        write_kernel,
        out_shape=(whole, whole),
        in_specs=[vmem, vmem],
        out_specs=(hbm, hbm),
        scratch_shapes=[pltpu.SemaphoreType.DMA((2, QX))],
        compiler_params=pltpu.CompilerParams(vmem_limit_bytes=4 * 2**20),
    )(
        pltpu.with_memory_space_constraint(f_new, pltpu.VMEM),
        pltpu.with_memory_space_constraint(g_new, pltpu.VMEM),
    )


def solution(mesh):
    return jax.shard_map(
        on_device,
        mesh=mesh,
        in_specs=(P(None, "gx", "gy", None), P(None, "gx", "gy", None), P()),
        out_specs=(P(None, "gx", "gy", None), P(None, "gx", "gy", None)),
        check_vma=False,
    )
```

```python
import jax
import jax.numpy as jnp
from jax import lax
from jax.experimental import pallas as pl
from jax.experimental.pallas import tpu as pltpu
from jax.sharding import PartitionSpec as P

lattice_velocity = [
    (0, 0, 0),
    (1, 0, 0),
    (-1, 0, 0),
    (0, 1, 0),
    (0, -1, 0),
    (0, 0, 1),
    (0, 0, -1),
    (1, 1, 0),
    (-1, -1, 0),
    (1, -1, 0),
    (-1, 1, 0),
    (1, 0, 1),
    (-1, 0, -1),
    (1, 0, -1),
    (-1, 0, 1),
    (0, 1, 1),
    (0, -1, -1),
    (0, 1, -1),
    (0, -1, 1),
]
plane_speed = 0.04
rising = [1, 7, 9, 11, 13]
northward = [3, 7, 10, 15, 17]
southward = [4, 8, 9, 16, 18]
level = [c for c in range(19) if lattice_velocity[c][0] == 0]
pairs = [1, 3, 5, 7, 9, 11, 13, 15, 17]
QX, QY, QZ = 8, 16, 512
NGX, NGY = 8, 16
MESH = pl.DeviceIdType.MESH


def axis_sum(direction, parts):
    total = None
    for sign, part in zip(direction, parts):
        if sign == 0:
            continue
        if total is None:
            total = part if sign > 0 else -part
        else:
            total = total + part if sign > 0 else total - part
    return total


def streamed(v, step_y, step_z):
    if step_z:
        v = pltpu.roll(v, step_z % QZ, 1)
    if step_y:
        v = pltpu.roll(v, step_y % QY, 0)
    return v


def step_kernel(
    off_hbm, f_hbm, g_hbm, fo, go,
    off_ref, fin, gin, ph, wp, yps, yp, mm, sb, ob, oc, wb, we, ce, ys, yr,
    load_sem, off_sem, send_sem, recv_sem,
):
    gx, gy = lax.axis_index("gx"), lax.axis_index("gy")
    odd = lax.rem(gx, 2)
    is_odd = odd == 1
    flat_gx = gx + 1 - 2 * odd
    plane_gx = lax.rem(gx + 2 * odd + NGX - 1, NGX)
    ring = lambda v: lax.rem(v + 2 * NGY, NGY)
    north, south = ring(gy + 1), ring(gy - 1)
    main_gy, extra_gy = ring(gy + 8), ring(gy + 9 - 18 * odd)
    core_gy = gy + 1 - 2 * lax.rem(gy, 2)
    sends_twice = lax.rem(gx + gy, 2) == 1
    to_hi, to_lo = ring(gy + 10 - 17 * odd), ring(gy + 7 - 17 * odd)
    partners = [
        (gx, north), (gx, south),
        (flat_gx, gy), (flat_gx, north), (flat_gx, south),
        (plane_gx, main_gy), (plane_gx, extra_gy), (plane_gx, to_hi), (plane_gx, to_lo),
    ]
    barrier = pltpu.get_barrier_semaphore()
    for partner in partners:
        pl.semaphore_signal(barrier, inc=1, device_id=partner, device_id_type=MESH)

    def load(which, x):
        source, target = ((g_hbm, gin), (f_hbm, fin))[which]
        return pltpu.make_async_copy(source.at[:, x], target.at[:, x], load_sem.at[which, x])

    for which in range(2):
        for x in (0, QX - 1, *range(1, QX - 1)):
            load(which, x).start()
    load_offsets = pltpu.make_async_copy(off_hbm, off_ref, off_sem)
    load_offsets.start()

    def remote(k, source, target, device):
        return pltpu.make_async_remote_copy(
            src_ref=source, dst_ref=target, send_sem=send_sem.at[k], recv_sem=recv_sem.at[k],
            device_id=device, device_id_type=MESH,
        )

    def phi_row(x, carry):
        load(0, x).wait()
        total = gin[0, x]
        for c in range(1, 19):
            total = total + gin[c, x]
        ph[x + 1] = total
        yps[0, pl.ds(x, 1), :] = total[QY - 1 : QY]
        yps[1, pl.ds(x, 1), :] = total[0:1]
        return carry

    phi_row(0, 0)
    phi_row(QX - 1, 0)
    flat_x, plane_x = 7 - 7 * odd, 7 * odd
    main_slot = 1 - odd
    phi_copies = [
        remote(0, ph.at[flat_x + 1], ph.at[9 * odd], (flat_gx, gy)),
        remote(1, ph.at[plane_x + 1], wp.at[main_slot], (plane_gx, main_gy)),
        remote(2, ph.at[plane_x + 1], wp.at[1 - main_slot], (plane_gx, extra_gy)),
        remote(3, yps.at[0], yp.at[0], (gx, north)),
        remote(4, yps.at[1], yp.at[1], (gx, south)),
    ]
    pl.semaphore_wait(barrier, len(partners))
    for copy in (phi_copies[1], phi_copies[2], phi_copies[0]):
        copy.start()
    lax.fori_loop(1, QX - 1, phi_row, 0)
    for copy in phi_copies[3:]:
        copy.start()

    load_offsets.wait()
    plane = lax.rem((gx + odd) // 2, 4)
    fraction = (2 * plane + 1).astype(jnp.float32) * 0.125
    near = jnp.where(is_odd, fraction, 1.0 - fraction)
    far = 1.0 - near
    rest = off_ref[plane] - 8 * QY
    first = jnp.where(is_odd, QY - 1 - rest, rest)

    def interpolated(window, start):
        count = window.shape[0]
        here = pltpu.roll(window, lax.rem(count - start, count), 0)
        return near * here[:QY] + far * pltpu.roll(here, count - 1, 0)[:QY]

    row_y = lax.broadcasted_iota(jnp.int32, (QY, QZ), 0)

    def gradients(x):
        centre, minus, plus = ph[x + 1], ph[x], ph[x + 2]
        south_v = jnp.where(row_y == 0, yp[0, pl.ds(x, 1), :], pltpu.roll(centre, 1, 0))
        north_v = jnp.where(row_y == QY - 1, yp[1, pl.ds(x, 1), :], pltpu.roll(centre, QY - 1, 0))
        upper, lower = pltpu.roll(centre, QZ - 1, 1), pltpu.roll(centre, 1, 1)
        lap = (plus + minus) + (north_v + south_v) + (upper + lower) - 6.0 * centre
        mu = centre * (0.0625 * centre * centre - 0.0625) - 0.04 * lap
        half = 0.5 * mu
        mm[0] = mu
        mm[1] = half * (plus - minus)
        mm[2] = half * (north_v - south_v)
        mm[3] = half * (upper - lower)

    def collide_row(x, face):
        gradients(x)
        if face is not None:
            top = odd == face
            sign = jnp.where(top, 1.0, -1.0)
            jump = sign * (-plane_speed)

        def chunk(step, carry):
            zs = pl.ds(pl.multiple_of(step * 128, 128), 128)
            for h in range(2):
                rows = pl.ds(8 * h, 8)
                read = lambda ref, c: ref[c, x, rows, zs]
                f = [read(fin, c) for c in range(19)]
                phi = ph[x + 1, rows, zs]
                mu = mm[0, rows, zs]
                force = [mm[a, rows, zs] for a in (1, 2, 3)]
                diff = {c: f[c] - f[c + 1] for c in pairs}
                rho = f[0]
                for c in pairs:
                    rho = rho + (f[c] + f[c + 1])
                inverse = 1.0 / rho
                velocity = []
                for a in range(3):
                    total = 0.5 * force[a]
                    for c in pairs:
                        s = lattice_velocity[c][a]
                        if s:
                            total = total + diff[c] if s > 0 else total - diff[c]
                    velocity.append(total * inverse)
                ux, uy, uz = velocity
                u2 = ux * ux + uy * uy + uz * uz
                uf = ux * force[0] + uy * force[1] + uz * force[2]
                base = 1.25 * rho * (1.0 - 1.5 * u2) - 1.125 * uf
                scale = 5.625 * rho
                pull = [3.375 * part for part in force]
                gbase = (10.0 / 9.0) * (3.0 * mu - 1.5 * phi * u2)
                gscale = 5.0 * phi
                fin[0, x, rows, zs] = (1.0 / 3.0) * base - 0.25 * f[0]
                gin[0, x, rows, zs] = (10.0 / 9.0) * (phi - 2.0 * mu - 0.5 * phi * u2) - (
                    1.0 / 9.0
                ) * read(gin, 0)
                if face == 1:
                    common = -3.0 * uy - 1.5 * jump
                    wrho, wphi = jump * rho, jump * phi
                for c in pairs:
                    w = 1.0 / 18.0 if c < 7 else 1.0 / 36.0
                    direction = lattice_velocity[c]
                    p = axis_sum(direction, velocity)
                    b = axis_sum(direction, pull)
                    a = scale * p
                    ab = a + b
                    even = w * (base + p * ab)
                    oddpart = (w / 3.0) * (a + ab)
                    f_up = (even + oddpart) - 0.25 * f[c]
                    f_down = (even - oddpart) - 0.25 * f[c + 1]
                    h_p = gscale * p
                    geven = w * (gbase + p * h_p)
                    godd = (2.0 * w / 3.0) * h_p
                    g_up = (geven + godd) - (1.0 / 9.0) * read(gin, c)
                    g_down = (geven - godd) - (1.0 / 9.0) * read(gin, c + 1)
                    fin[c, x, rows, zs] = f_up
                    fin[c + 1, x, rows, zs] = f_down
                    gin[c, x, rows, zs] = g_up
                    gin[c + 1, x, rows, zs] = g_down
                    if face is not None and c in rising:
                        j = rising.index(c)
                        f_sent = jnp.where(top, f_up, f_down)
                        g_sent = jnp.where(top, g_up, g_down)
                        if face == 1:
                            cy = float(direction[1])
                            delta = common
                            if cy:
                                delta = delta + (cy * 9.0 * p + (cy * 3.0 * sign + 4.5 * jump))
                            f_sent = f_sent + w * (wrho * delta)
                            g_sent = g_sent + w * (wphi * delta)
                        sb[face, j, rows, zs] = f_sent
                        sb[face, 5 + j, rows, zs] = g_sent
            return carry

        lax.fori_loop(0, QZ // 128, chunk, 0)
        slot = jnp.where(top, 1, 0) if face is not None else x + 1
        group, line = slot // 4, lax.rem(slot, 4) * 10
        for d, chosen, y in ((0, northward, QY - 1), (1, southward, 0)):
            for j, c in enumerate(chosen):
                ys[d, group, pl.ds(line + j, 1), :] = fin[c, x, y : y + 1, :]
                ys[d, group, pl.ds(line + 5 + j, 1), :] = gin[c, x, y : y + 1, :]
        if face is not None:
            j_hi = jnp.where(top, 1, 2)
            for family in range(2):
                ce[face, 0, family : family + 1, :] = sb[face, j_hi + 5 * family, QY - 1 : QY, :]
                ce[face, 1, family : family + 1, :] = sb[face, 3 - j_hi + 5 * family, 0:1, :]

    def wait_f(x, carry):
        load(1, x).wait()
        return carry

    lax.fori_loop(0, QX, wait_f, 0)

    for copy in (phi_copies[0], phi_copies[3], phi_copies[4]):
        copy.wait_recv()
    collide_row(flat_x, 0)
    flat_copies = [
        remote(5, sb.at[0, pl.ds(0, 4)], ob.at[pl.ds(0, 4)], (flat_gx, gy)),
        remote(6, ce.at[0, 0], oc.at[0], (flat_gx, north)),
        remote(7, ce.at[0, 1], oc.at[1], (flat_gx, south)),
    ]
    for copy in flat_copies:
        copy.start()
    phi_copies[1].wait_recv()
    phi_copies[2].wait_recv()
    ph[9 * odd] = interpolated(wp[...].reshape(2 * QY, QZ), first)
    collide_row(plane_x, 1)
    plane_copies = [
        remote(8, ce.at[1, 0], we.at[0], (plane_gx, to_hi)),
        remote(9, ce.at[1, 1], we.at[1], (plane_gx, to_lo)),
    ]
    rows_at = lambda half, slot: wb.at[pl.ds(5 * half, 5), pl.ds(8 + QY * slot, QY)]
    layer = lambda half: sb.at[1, pl.ds(5 * half, 5)]
    main_copies = [
        remote(10 + half, layer(half), rows_at(half, main_slot), (plane_gx, main_gy))
        for half in range(2)
    ]
    extra_copies = [
        remote(16 + half, layer(half), rows_at(half, 1 - main_slot), (plane_gx, extra_gy))
        for half in range(2)
    ]
    hand_on = [
        pltpu.make_async_remote_copy(
            src_ref=rows_at(half, odd), dst_ref=rows_at(half, 1 - odd),
            send_sem=send_sem.at[19 + half], recv_sem=recv_sem.at[16 + half],
            device_id=(gx, core_gy), device_id_type=MESH,
        )
        for half in range(2)
    ]
    for copy in plane_copies + main_copies:
        copy.start()

    @pl.when(sends_twice)
    def _():
        for copy in extra_copies:
            copy.start()

    def inner_row(x, carry):
        collide_row(x, None)
        return carry

    side_copies = [
        remote(12 + 2 * d + group, ys.at[d, group], yr.at[d, group], (gx, (north, south)[d]))
        for group in range(2)
        for d in range(2)
    ]
    lax.fori_loop(1, 3, inner_row, 0)
    side_copies[0].start()
    side_copies[1].start()
    lax.fori_loop(3, QX - 1, inner_row, 0)
    side_copies[2].start()
    side_copies[3].start()

    families = ((fin, fo), (gin, go))

    def stream_level(x, carry):
        for source, target in families:
            for c in level:
                target[c, x] = streamed(source[c, x], *lattice_velocity[c][1:])
        return carry

    def stream_across(x, carry):
        for source, target in families:
            for c in rising:
                _, step_y, step_z = lattice_velocity[c]
                target[c, x + 1] = streamed(source[c, x], step_y, step_z)
                target[c + 1, x] = streamed(source[c + 1, x + 1], -step_y, -step_z)
        return carry

    flat_copies.append(remote(18, sb.at[0, pl.ds(4, 6)], ob.at[pl.ds(4, 6)], (flat_gx, gy)))
    flat_copies[-1].start()
    lax.fori_loop(0, QX, stream_level, 0)
    lax.fori_loop(0, QX - 1, stream_across, 0)

    for copy in side_copies:
        copy.wait_recv()

    def side_line(x):
        slot = jnp.where(x == 0, 0, jnp.where(x == QX - 1, 1, x + 1))
        return slot // 4, lax.rem(slot, 4) * 10

    def side_rows(x, chosen_x, shift):
        group, line = side_line(x)
        for d, chosen, y in ((0, northward, 0), (1, southward, QY - 1)):
            for j, c in enumerate(chosen):
                step_x, _, step_z = lattice_velocity[c]
                if step_x != chosen_x:
                    continue
                for family in range(2):
                    row = yr[d, group, pl.ds(line + 5 * family + j, 1), :]
                    if step_z:
                        row = pltpu.roll(row, step_z % QZ, 1)
                    families[family][1][c, x + shift, y : y + 1, :] = row

    def side_level(x, carry):
        side_rows(x, 0, 0)
        return carry

    def side_across(x, carry):
        side_rows(x, 1, 1)
        side_rows(x + 1, -1, -1)
        return carry

    lax.fori_loop(0, QX, side_level, 0)
    lax.fori_loop(0, QX - 1, side_across, 0)

    for half in range(2):
        main_copies[half].wait_recv()
        pl.when(sends_twice)(hand_on[half].start)

    for copy in flat_copies:
        copy.wait_recv()

    def arrive_flat(sign, x):
        for j, c in enumerate(rising):
            step_y, step_z = sign * lattice_velocity[c][1], sign * lattice_velocity[c][2]
            c = c if sign > 0 else c + 1
            for family in range(2):
                v = streamed(ob[5 * family + j], step_y, step_z)
                if step_y > 0:
                    v = jnp.where(row_y == 0, oc[0, family : family + 1, :], v)
                elif step_y < 0:
                    v = jnp.where(row_y == QY - 1, oc[1, family : family + 1, :], v)
                families[family][1][c, x] = v

    pl.when(is_odd)(lambda: arrive_flat(1, 0))
    pl.when(jnp.logical_not(is_odd))(lambda: arrive_flat(-1, QX - 1))

    for copy in plane_copies + extra_copies:
        copy.wait_recv()

    def arrive_plane(sign, x):
        for j, c in enumerate(rising):
            step_y, step_z = sign * lattice_velocity[c][1], sign * lattice_velocity[c][2]
            c = c if sign > 0 else c + 1
            for family in range(2):
                k = 5 * family + j
                if step_y > 0:
                    wb[k, 7:8, :] = we[0, family : family + 1, :]
                elif step_y < 0:
                    wb[k, 8 + 2 * QY : 9 + 2 * QY, :] = we[1, family : family + 1, :]
                v = interpolated(wb[k], first + (8 - step_y))
                families[family][1][c, x] = streamed(v, 0, step_z)

    pl.when(jnp.logical_not(is_odd))(lambda: arrive_plane(1, 0))
    pl.when(is_odd)(lambda: arrive_plane(-1, QX - 1))

    for copy in phi_copies + flat_copies + plane_copies + main_copies + side_copies:
        copy.wait_send()

    @pl.when(sends_twice)
    def _():
        for copy in extra_copies + hand_on:
            copy.wait_send()


def write_kernel(f, g, f_hbm, g_hbm, sem):
    copies = [
        pltpu.make_async_copy(source.at[:, x], target.at[:, x], sem.at[which, x])
        for x in range(QX)
        for which, (source, target) in enumerate(((f, f_hbm), (g, g_hbm)))
    ]
    for copy in copies:
        copy.start()
    for copy in copies:
        copy.wait()


def on_device(momentum_dist, order_dist, offsets):
    block = (19, QX, QY, QZ)
    f32 = jnp.float32
    vmem, hbm = pl.BlockSpec(memory_space=pltpu.VMEM), pl.BlockSpec(memory_space=pltpu.HBM)
    f_new, g_new = pl.pallas_call(
        step_kernel,
        out_shape=(pltpu.VMEM(block, f32), pltpu.VMEM(block, f32)),
        in_specs=[hbm, hbm, hbm],
        out_specs=(vmem, vmem),
        scratch_shapes=[
            pltpu.SMEM((4,), jnp.int32),
            pltpu.VMEM(block, f32),
            pltpu.VMEM(block, f32),
            pltpu.VMEM((QX + 2, QY, QZ), f32),
            pltpu.VMEM((2, QY, QZ), f32),
            pltpu.VMEM((2, QX, QZ), f32),
            pltpu.VMEM((2, QX, QZ), f32),
            pltpu.VMEM((4, QY, QZ), f32),
            pltpu.VMEM((2, 10, QY, QZ), f32),
            pltpu.VMEM((10, QY, QZ), f32),
            pltpu.VMEM((2, 2, QZ), f32),
            pltpu.VMEM((10, 2 * QY + 16, QZ), f32),
            pltpu.VMEM((2, 2, QZ), f32),
            pltpu.VMEM((2, 2, 2, QZ), f32),
            pltpu.VMEM((2, 2, 40, QZ), f32),
            pltpu.VMEM((2, 2, 40, QZ), f32),
            pltpu.SemaphoreType.DMA((2, QX)),
            pltpu.SemaphoreType.DMA,
            pltpu.SemaphoreType.DMA((21,)),
            pltpu.SemaphoreType.DMA((19,)),
        ],
        compiler_params=pltpu.CompilerParams(
            collective_id=0, has_side_effects=True, vmem_limit_bytes=32 * 2**20
        ),
    )(
        *(
            pltpu.with_memory_space_constraint(operand, pltpu.HBM)
            for operand in (offsets, momentum_dist, order_dist)
        )
    )
    whole = jax.ShapeDtypeStruct(block, f32)
    return pl.pallas_call(
        write_kernel,
        out_shape=(whole, whole),
        in_specs=[vmem, vmem],
        out_specs=(hbm, hbm),
        scratch_shapes=[pltpu.SemaphoreType.DMA((2, QX))],
        compiler_params=pltpu.CompilerParams(vmem_limit_bytes=4 * 2**20),
    )(
        pltpu.with_memory_space_constraint(f_new, pltpu.VMEM),
        pltpu.with_memory_space_constraint(g_new, pltpu.VMEM),
    )


def solution(mesh):
    return jax.shard_map(
        on_device,
        mesh=mesh,
        in_specs=(P(None, "gx", "gy", None), P(None, "gx", "gy", None), P()),
        out_specs=(P(None, "gx", "gy", None), P(None, "gx", "gy", None)),
        check_vma=False,
    )
```
